768 devices in a mesh: rows: 32 (over y, z_hi, core), cols: 24 (over x, z_lo).
Axes of the slice: x: 4, y: 8, z: 12 (z_hi: 2, z_lo: 6; z = z_hi * 6 + z_lo), core: 2. Of those that a mesh axis runs over, the one named last changes fastest.
Arguments:
- tokens: bfloat16 [256, 384, 512], P('rows', 'cols'), may hold values from -6 to 6
- cotangent: bfloat16 [256, 384, 512], P('rows', 'cols'), may hold values from -6 to 6
- region: int32 [256, 384], P('rows', 'cols'), may hold values from 0 to 1
- norm_gain: float32 [512], replicated, may hold values from 0.5 to 1.5
- qkv_weight: bfloat16 [512, 1536], replicated, may hold values from -0.25 to 0.25
- out_weight: bfloat16 [512, 512], replicated, may hold values from -0.25 to 0.25
- bias_table: float32 [225, 16], replicated, may hold values from -2 to 203
- bias_bucket: int32 [64, 64], replicated, may hold values from 0 to 224
Outputs:
- grad_tokens: bfloat16 [256, 384, 512], P('rows', 'cols')
- grad_qkv: float32 [512, 1536], P('rows', 'cols')
- grad_out_weight: float32 [512, 512], P('rows')
- grad_gain: float32 [512], replicated
- grad_bias_table: float32 [225, 16], replicated
The draws below stay inside these ranges and needn't reach their ends.
All inputs are finite; a program needn't handle non-finite values.
Results may differ from the reference program's by a relative error of at most 0.033.
Values may be sent and summed in bfloat16 or wider, within the bound.
No kernel may reach another device: no remote copies, remote signals or barrier semaphores. Data moves between devices by JAX's collectives and lax.ppermute only.
A program may use at most 64 MiB of HBM per device.

```python
import jax
import jax.numpy as jnp
from jax import lax

D = 512
HEADS = 16
WIN = 8
SHIFT = 4
NBIAS = 225
NR = 256
NC = 384


def draw_bias_table(key, part):
    base_key = jax.random.fold_in(jax.random.fold_in(key, 17), 0)
    base_values = jax.random.uniform(base_key, (NBIAS, HEADS), jnp.float32, -2.0, 2.0)
    return base_values


def with_ends(drawn, rng, smallest, largest):
    shape = drawn.shape
    place = [jax.random.randint(jax.random.fold_in(rng, axis), (), 0, shape[axis]) for axis in range(len(shape))]
    drawn = drawn.at[tuple(place)].set(smallest)
    longest = shape.index(max(shape))
    place[longest] = (place[longest] + 1) % shape[longest]
    return drawn.at[tuple(place)].set(largest)


def shard_levels(own_key, dims, cuts, low, largest):
    loudness = 1.0
    for dim, blocks in cuts:
        heights = jax.random.uniform(jax.random.fold_in(jax.random.fold_in(own_key, 6), dim), (blocks,), jnp.float32, low / len(cuts), largest / len(cuts))
        loudness = loudness * jnp.repeat(jnp.exp(heights), dims[dim] // blocks).reshape((-1,) + (1,) * (len(dims) - 1 - dim))
    return loudness


def normal_values(own_key, shape, deviation, limit, shards=(), kind=jnp.bfloat16):
    drawn = jax.random.normal(own_key, shape, jnp.float32) * deviation
    if len(shards) > 0:
        drawn = shard_levels(own_key, shape, shards, -0.22, 0.18) * drawn
    return jnp.clip(drawn, min=-limit, max=limit).astype(kind)


def setup_inputs(seed: int = 0) -> dict:
    streams_of = jax.random.split(jax.random.key(seed), 9)
    tokens = normal_values(streams_of[0], (NR, NC, D), 1.0, 6.0, ((0, 32), (1, 24)))
    cotangent = normal_values(streams_of[1], (NR, NC, D), 1.0, 6.0, ((0, 32), (1, 24)))
    region = with_ends(jax.random.randint(streams_of[2], (NR, NC), 0, 2), jax.random.fold_in(streams_of[2], 1), 0, 1).astype(jnp.int32)
    norm_gain = jnp.clip(1.0 + 0.1 * jax.random.normal(streams_of[3], (D,), jnp.float32), 0.5, 1.5)
    qkv_weight = normal_values(streams_of[4], (D, 3 * D), D ** -0.5, 0.25)
    out_weight = normal_values(streams_of[5], (D, D), D ** -0.5, 0.25)
    bias_table = draw_bias_table(jax.random.fold_in(streams_of[8], 71), 0)
    bias_bucket = with_ends(jax.random.randint(streams_of[7], (WIN * WIN, WIN * WIN), 0, NBIAS), jax.random.fold_in(streams_of[7], 1), 0, NBIAS - 1).astype(jnp.int32)
    return dict(tokens=tokens, cotangent=cotangent, region=region, norm_gain=norm_gain, qkv_weight=qkv_weight, out_weight=out_weight, bias_table=bias_table, bias_bucket=bias_bucket)


EPSILON = 1e-05

def layer_stats(values):
    floats = values.astype(jnp.float32)
    average = lax.optimization_barrier(jnp.mean(floats, axis=-1, keepdims=True))
    centred = floats - average
    variance = lax.optimization_barrier(jnp.mean(centred * centred, axis=-1, keepdims=True))
    inv_std = lax.rsqrt(variance + EPSILON)
    return (centred * inv_std, inv_std)

def window_core(normed, grad_out, labels, flags, qkv_weight, out_weight, bias):
    count = normed.shape[0]
    width = normed.shape[2]
    head_dim = width // HEADS
    scale = head_dim ** (-0.5)
    area = WIN * WIN
    packed = jnp.dot(normed.reshape(-1, width), qkv_weight, preferred_element_type=jnp.float32).astype(jnp.bfloat16)
    packed = packed.reshape(count, area, 3, HEADS, head_dim).transpose(2, 0, 3, 1, 4)
    query_heads = packed[0].astype(jnp.float32)
    key_heads = packed[1].astype(jnp.float32)
    value_heads = packed[2].astype(jnp.float32)
    allowed = (labels[:, :, None] == labels[:, None, :]) & (flags[:, :, None] == flags[:, None, :])
    scores = jnp.einsum('whqd,whkd->whqk', query_heads, key_heads) * scale + bias[None]
    scores = jnp.where(allowed[:, None], scores, -1e+30)
    raised = jnp.exp(scores - lax.optimization_barrier(jnp.max(scores, axis=-1, keepdims=True)))
    probs = raised / lax.optimization_barrier(jnp.sum(raised, axis=-1, keepdims=True))
    probs_low = probs.astype(jnp.bfloat16).astype(jnp.float32)
    attended = jnp.einsum('whqk,whkd->whqd', probs_low, value_heads).astype(jnp.bfloat16)
    attended_flat = attended.transpose(0, 2, 1, 3).reshape(count, area, width)
    grad_attended = jnp.dot(grad_out.reshape(-1, width), out_weight.T, preferred_element_type=jnp.float32).astype(jnp.bfloat16)
    grad_attended = grad_attended.reshape(count, area, HEADS, head_dim).transpose(0, 2, 1, 3).astype(jnp.float32)
    grad_probs = jnp.einsum('whqd,whkd->whqk', grad_attended, value_heads)
    grad_values = jnp.einsum('whqk,whqd->whkd', probs_low, grad_attended).astype(jnp.bfloat16)
    grad_scores = probs * (grad_probs - lax.optimization_barrier(jnp.sum(probs * grad_probs, axis=-1, keepdims=True)))
    grad_scaled = (grad_scores * scale).astype(jnp.bfloat16).astype(jnp.float32)
    grad_queries = jnp.einsum('whqk,whkd->whqd', grad_scaled, key_heads).astype(jnp.bfloat16)
    grad_keys = jnp.einsum('whqk,whqd->whkd', grad_scaled, query_heads).astype(jnp.bfloat16)
    grad_packed = jnp.stack([grad_queries, grad_keys, grad_values], axis=0).transpose(1, 3, 0, 2, 4).reshape(count, area, 3 * width)
    grad_normed = jnp.dot(grad_packed.reshape(-1, 3 * width), qkv_weight.T, preferred_element_type=jnp.float32).reshape(count, area, width)
    return (grad_normed, attended_flat, grad_packed, grad_scores)

def to_bands(array):
    trailing = array.shape[2:]
    blocked = array.reshape((NR // WIN, WIN, NC // WIN, WIN) + trailing)
    order = (0, 2, 1, 3) + tuple(range(4, 4 + len(trailing)))
    return blocked.transpose(order).reshape((NR // WIN, NC // WIN, WIN * WIN) + trailing)

def reference(tokens, cotangent, region, norm_gain, qkv_weight, out_weight, bias_table, bias_bucket):
    width = tokens.shape[2]
    token_hat, inv_std = layer_stats(tokens)
    normed = (token_hat * norm_gain).astype(jnp.bfloat16)
    flag_rows = (jnp.arange(NR, dtype=jnp.int32) < SHIFT).astype(jnp.int32)
    flags = jnp.broadcast_to(flag_rows[:, None], (NR, NC))
    rolled_normed = jnp.roll(normed, (-SHIFT, -SHIFT), axis=(0, 1))
    rolled_cot = jnp.roll(cotangent, (-SHIFT, -SHIFT), axis=(0, 1))
    rolled_region = jnp.roll(region, (-SHIFT, -SHIFT), axis=(0, 1))
    rolled_flags = jnp.roll(flags, (-SHIFT, -SHIFT), axis=(0, 1))
    bias = bias_table[bias_bucket].transpose(2, 0, 1)

    def band_step(carry, inputs):
        sum_qkv, sum_out, pair_sum = carry
        band_normed, band_cot, band_region, band_flags = inputs
        grad_normed, attended, grad_packed, grad_scores = window_core(band_normed, band_cot, band_region, band_flags, qkv_weight, out_weight, bias)
        sum_qkv = sum_qkv + jnp.dot(band_normed.reshape(-1, width).T, grad_packed.reshape(-1, 3 * width), preferred_element_type=jnp.float32)
        sum_out = sum_out + jnp.dot(attended.reshape(-1, width).T, band_cot.reshape(-1, width), preferred_element_type=jnp.float32)
        pair_sum = pair_sum + lax.optimization_barrier(jnp.sum(grad_scores, axis=0))
        return ((sum_qkv, sum_out, pair_sum), grad_normed)
    start_carry = (jnp.zeros((width, 3 * width), jnp.float32), jnp.zeros((width, width), jnp.float32), jnp.zeros((HEADS, WIN * WIN, WIN * WIN), jnp.float32))
    carried, grad_bands = lax.scan(band_step, start_carry, (to_bands(rolled_normed), to_bands(rolled_cot), to_bands(rolled_region), to_bands(rolled_flags)))
    grad_qkv, grad_out_weight, pair_sum = carried
    grad_rolled = grad_bands.reshape(NR // WIN, NC // WIN, WIN, WIN, width).transpose(0, 2, 1, 3, 4).reshape(NR, NC, width)
    grad_normed = jnp.roll(grad_rolled, (SHIFT, SHIFT), axis=(0, 1))
    grad_bias_table = jax.ops.segment_sum(pair_sum.reshape(HEADS, -1).T, bias_bucket.reshape(-1), NBIAS)
    grad_gain = lax.optimization_barrier(jnp.sum(grad_normed * token_hat, axis=(0, 1)))
    grad_hat = grad_normed * norm_gain
    grad_tokens = cotangent.astype(jnp.float32) + inv_std * (grad_hat - lax.optimization_barrier(jnp.mean(grad_hat, axis=-1, keepdims=True)) - token_hat * lax.optimization_barrier(jnp.mean(grad_hat * token_hat, axis=-1, keepdims=True)))
    return (grad_tokens.astype(jnp.bfloat16), grad_qkv, grad_out_weight, grad_gain, grad_bias_table)
```

```python
import jax
import jax.numpy as jnp
from jax import lax
from jax.experimental import pallas as pl
from jax.experimental.pallas import tpu as pltpu
from jax.sharding import Mesh
from jax.sharding import PartitionSpec as P

D = 512
HEADS = 16
HEAD_DIM = 32
WIN = 8
SHIFT = 4
NBIAS = 225
AREA = WIN * WIN
TOKENS = 128
GROUP = 4
SCALE = HEAD_DIM ** (-0.5)
EPSILON = 1e-05

F32 = jnp.float32
BF16 = jnp.bfloat16

PARTS = (("y", 8), ("zh", 2), ("core", 2), ("x", 4), ("zl", 6))
ROWS = ("y", "zh", "core")
COLS = ("x", "zl")
NROWS = 32
NCOLS = 24

ANY_PARAMS = pltpu.CompilerParams(vmem_limit_bytes=48 * 1024 * 1024)


def dot(a, b):
    return lax.dot_general(a, b, (((1,), (0,)), ((), ())), preferred_element_type=F32)


def dot_nt(a, b):
    return lax.dot_general(a, b, (((1,), (1,)), ((), ())), preferred_element_type=F32)


def dot_tn(a, b):
    return lax.dot_general(a, b, (((0,), (0,)), ((), ())), preferred_element_type=F32)


def iota(shape, dim):
    return lax.broadcasted_iota(jnp.int32, shape, dim)


def split_high_low(value):
    high = value.astype(BF16)
    low = (value - high.astype(F32)).astype(BF16)
    return high, low


def layer_stats(floats):
    average = jnp.mean(floats, axis=-1, keepdims=True)
    centred = floats - average
    variance = jnp.mean(centred * centred, axis=-1, keepdims=True)
    inv_std = lax.rsqrt(variance + EPSILON)
    return centred * inv_std, inv_std


def pack_kernel(tok, cot, reg, to_up, to_left, to_diag):
    to_up[8] = jnp.zeros((12, D), BF16)
    to_left[8] = jnp.zeros((4, D), BF16)
    to_diag[8] = jnp.zeros((4, D), BF16)
    for k, src in ((0, tok), (4, cot)):
        for r in range(SHIFT):
            top = src[r].astype(F32)
            low = src[SHIFT + r].astype(F32)
            to_up[k + r] = top[4:16].astype(BF16)
            to_diag[k + r] = top[0:4].astype(BF16)
            to_left[k + r] = low[0:4].astype(BF16)
    labels = reg[...].astype(F32)
    to_up[8, 0:4, 0:16] = labels[0:4].astype(BF16)
    to_diag[8, 0:4, 0:16] = labels[0:4].astype(BF16)
    to_left[8, 0:4, 0:16] = labels[4:8].astype(BF16)


def bias_kernel(table, bucket, bias, bucket2, padded):
    padded[...] = jnp.zeros_like(padded)
    padded[0:NBIAS, 0:HEADS] = table[...]
    turned = padded[...].T
    both = jnp.concatenate([bucket[...], bucket[...]], axis=1)
    bucket2[...] = both
    for block in range(AREA // 8):
        index = both[block * 8 : block * 8 + 8]
        upper = index >= 128
        within = jnp.bitwise_and(index, 127)
        for h in range(HEADS):
            first = jnp.broadcast_to(turned[h : h + 1, 0:128], (8, 128))
            second = jnp.broadcast_to(turned[h : h + 1, 128:256], (8, 128))
            got_first = jnp.take_along_axis(first, within, axis=1, mode="promise_in_bounds")
            got_second = jnp.take_along_axis(second, within, axis=1, mode="promise_in_bounds")
            bias[h, block * 8 : block * 8 + 8, :] = jnp.where(upper, got_second, got_first)


def window_kernel(
    tok, cot, reg, up, left, diag, gain, wqkv, wout, bias, bucket2,
    send, keep, own_grad, down_grad, right_grad, diag_grad,
    frame_t, frame_c, labels, packed, attended, grad_att, pairs, grad_in,
):
    for src, k, frame in ((tok, 0, frame_t), (cot, 4, frame_c)):
        for r in range(SHIFT):
            own = src[SHIFT + r].astype(F32)
            frame[r * 8 : r * 8 + 8, :] = own[4:12]
            frame[64 + r * 8 : 64 + r * 8 + 4, :] = own[12:16]
            frame[64 + r * 8 + 4 : 64 + r * 8 + 8, :] = left[k + r].astype(F32)
            s = SHIFT + r
            below = up[k + r].astype(F32)
            frame[s * 8 : s * 8 + 8, :] = below[0:8]
            frame[64 + s * 8 : 64 + s * 8 + 4, :] = below[8:12]
            frame[64 + s * 8 + 4 : 64 + s * 8 + 8, :] = diag[k + r].astype(F32)

    mine = reg[...].astype(F32)
    labels[...] = jnp.zeros_like(labels)
    labels[0:4, 0:12] = mine[4:8, 4:16]
    labels[0:4, 12:16] = left[8, 0:4, 0:16].astype(F32)[:, 0:4]
    labels[4:8, 0:12] = up[8, 0:4, 0:16].astype(F32)[:, 4:16]
    labels[4:8, 12:16] = diag[8, 0:4, 0:16].astype(F32)[:, 0:4]
    row_tile = (lax.axis_index("y") * 2 + lax.axis_index("zh")) * 2 + lax.axis_index("core")
    last = (row_tile == NROWS - 1).astype(F32)
    flags = jnp.where(iota((8, 128), 0) >= 4, 2.0, 0.0) * last
    coded = labels[...] + flags + jnp.where(iota((8, 128), 1) >= 8, 4.0, 0.0)
    token_lane = iota((128, 128), 1)
    token_row = iota((128, 128), 0)

    def column_of(token):
        return (token // 64) * 8 + token % 8

    def row_of(token):
        return (token // 8) % 8

    pick_lane = (column_of(token_lane) == token_row).astype(BF16)
    wide = dot(coded.astype(BF16), pick_lane)
    code_row = jnp.sum(
        jnp.where(row_of(iota((8, 128), 1)) == iota((8, 128), 0), wide, 0.0), axis=0, keepdims=True
    )
    pick_row = (column_of(token_row) == token_lane).astype(BF16)
    padded_codes = jnp.concatenate([coded, jnp.zeros((120, 128), F32)], axis=0).astype(BF16)
    tall = dot_nt(pick_row, padded_codes)
    code_col = jnp.sum(
        jnp.where(row_of(token_row) == token_lane, tall, 0.0), axis=1, keepdims=True
    )
    allowed = jnp.broadcast_to(code_col, (128, 128)) == jnp.broadcast_to(code_row, (128, 128))
    allowed4 = jnp.concatenate([allowed.astype(F32)] * GROUP, axis=0) > 0.5

    hat, _ = layer_stats(frame_t[...])
    normed = (hat * gain[...]).astype(BF16)
    cots = frame_c[...].astype(BF16)
    packed[...] = dot(normed, wqkv[...]).astype(BF16)
    grad_att[...] = dot_nt(cots, wout[...]).astype(BF16)
    send[0:TOKENS, 3 * D : 4 * D] = cots

    lane_head = iota((TOKENS, 128), 1) // HEAD_DIM
    masks = [lane_head == h for h in range(GROUP)]

    def stacked(value):
        return jnp.concatenate(
            [jnp.where(m, value, jnp.zeros_like(value)) for m in masks], axis=0
        )

    def beside(value):
        return jnp.concatenate([value[h * 128 : h * 128 + 128] for h in range(GROUP)], axis=1)

    for g in range(HEADS // GROUP):
        at = g * 128
        query = packed[:, at : at + 128]
        key = packed[:, D + at : D + at + 128]
        value = packed[:, 2 * D + at : 2 * D + at + 128]
        outer = grad_att[:, at : at + 128]
        query_s = stacked(query)
        outer_s = stacked(outer)
        biases = []
        for h in range(GROUP):
            one = bias[g * GROUP + h]
            biases += [one, one]
        scores = dot_nt(query_s, key) * SCALE + jnp.concatenate(biases, axis=0)
        scores = jnp.where(allowed4, scores, -1e30)
        raised = jnp.exp(scores - jnp.max(scores, axis=-1, keepdims=True))
        probs = raised / jnp.sum(raised, axis=-1, keepdims=True)
        probs_low = probs.astype(BF16)
        grad_probs = dot_nt(outer_s, value)
        inner = probs * grad_probs
        grad_scores = probs * (grad_probs - jnp.sum(inner, axis=-1, keepdims=True))
        grad_scaled = (grad_scores * SCALE).astype(BF16)
        attended[:, at : at + 128] = dot(beside(probs_low), stacked(value)).astype(BF16)
        send[0:TOKENS, at : at + 128] = dot(beside(grad_scaled), stacked(key)).astype(BF16)
        send[0:TOKENS, D + at : D + at + 128] = dot_tn(grad_scaled, query_s).astype(BF16)
        send[0:TOKENS, 2 * D + at : 2 * D + at + 128] = dot_tn(probs_low, outer_s).astype(BF16)
        for h in range(GROUP):
            one = grad_scores[h * 128 : h * 128 + 128]
            pairs[g * GROUP + h] = one[0:64] + one[64:128]

    core = lax.axis_index("core")
    for k, matrix in ((0, normed), (1, attended[...])):
        turned = matrix.astype(F32).T.reshape(16, 2, 16, TOKENS)
        even, odd = turned[:, 0].reshape(256, TOKENS), turned[:, 1].reshape(256, TOKENS)
        kept = jnp.where(core == 0, even, odd).astype(BF16)
        sent = jnp.where(core == 0, odd, even).astype(BF16)
        for b in range(2):
            lane = (2 * k + b) * 128
            keep[:, lane : lane + 128] = kept[b * 128 : b * 128 + 128]
            send[0:TOKENS, 4 * D + lane : 4 * D + lane + 128] = sent[b * 128 : b * 128 + 128]

    grad_normed = dot_nt(send[0:TOKENS, 0 : 3 * D], wqkv[...])
    grad_in[...] = grad_normed
    gain_sum = jnp.sum(grad_normed * hat, axis=0, keepdims=True)

    bucket_of = iota((256, 128), 0)

    def add_row(i, total):
        high, low = split_high_low(pairs[:, i, :])
        hot = (bucket_of == jnp.broadcast_to(bucket2[pl.ds(i, 1), :], (256, 128))).astype(BF16)
        return total + dot_nt(jnp.concatenate([high, low], axis=0), hot)

    sums = lax.fori_loop(0, AREA, add_row, jnp.zeros((2 * HEADS, 256), F32), unroll=8)
    table = sums[0:HEADS] + sums[HEADS : 2 * HEADS]
    high, low = split_high_low(table)
    send[TOKENS : TOKENS + 16, 0:256] = high
    send[TOKENS : TOKENS + 16, 256:512] = low
    high, low = split_high_low(jnp.concatenate([gain_sum, jnp.zeros((15, D), F32)], axis=0))
    send[TOKENS : TOKENS + 16, 512:1024] = high
    send[TOKENS : TOKENS + 16, 1024:1536] = low
    send[TOKENS : TOKENS + 16, 1536:2560] = jnp.zeros((16, 1024), BF16)

    for r in range(SHIFT):
        s = SHIFT + r
        own_grad[r, 0:8, :] = grad_in[r * 8 : r * 8 + 8, :]
        own_grad[r, 8:12, :] = grad_in[64 + r * 8 : 64 + r * 8 + 4, :]
        right_grad[r] = grad_in[64 + r * 8 : 64 + r * 8 + 8, :][4:8].astype(BF16)
        down_grad[r] = jnp.concatenate(
            [grad_in[s * 8 : s * 8 + 8, :], grad_in[64 + s * 8 : 64 + s * 8 + 8, :][0:4]], axis=0
        ).astype(BF16)
        diag_grad[r] = grad_in[64 + s * 8 : 64 + s * 8 + 8, :][4:8].astype(BF16)


def product_kernel(mine, other, keep, out):
    def rows(block):
        lane = block * 128
        return jnp.concatenate(
            [keep[:, lane : lane + 128], other[0:TOKENS, 4 * D + lane : 4 * D + lane + 128]], axis=1
        )

    right = jnp.concatenate([mine[0:TOKENS, 0 : 4 * D], other[0:TOKENS, 0 : 4 * D]], axis=0)
    for half in range(2):
        qkv = dot(rows(half), right[:, 0 : 3 * D]).astype(BF16)
        proj = dot(rows(2 + half), right[:, 3 * D : 4 * D]).astype(BF16)
        for k in range(4):
            y = half * 4 + k
            for x in range(4):
                out[y, x, :, 0:384] = qkv[k * 32 : k * 32 + 32, x * 384 : x * 384 + 384]
                out[y, x, :, 384:512] = proj[k * 32 : k * 32 + 32, x * 128 : x * 128 + 128]
    small = mine[TOKENS : TOKENS + 16, 0:1536].astype(F32) + other[TOKENS : TOKENS + 16, 0:1536].astype(F32)
    table = small[:, 0:256] + small[:, 256:512]
    gain = small[0:8, 512:1024] + small[0:8, 1024:1536]
    for x in range(4):
        part = jnp.concatenate(
            [
                table[4 * x : 4 * x + 4, 0:128],
                table[4 * x : 4 * x + 4, 128:256],
                gain[:, x * 128 : x * 128 + 128],
            ],
            axis=0,
        )
        high, low = split_high_low(part)
        both = jnp.concatenate([high, low], axis=0)
        for y in range(8):
            out[y, x, :, 512:640] = both


def plane_sum_kernel(parts, out):
    total = jnp.sum(parts[...].astype(F32), axis=0)
    small = (total[0:16, 512:640] + total[16:32, 512:640]).astype(BF16)
    for zh in range(2):
        rows = total[zh * 16 : zh * 16 + 16]
        proj = rows[:, 384:512].astype(BF16)
        for zl in range(6):
            lane = (zl // 2) * 128
            qkv = rows[:, lane : lane + 128]
            if zl % 2 == 1:
                qkv = pltpu.roll(qkv, 64, 1)
            out[zh * 6 + zl, :, 0:128] = proj
            out[zh * 6 + zl, :, 128:256] = qkv.astype(BF16)
            out[zh * 6 + zl, :, 256:384] = small


def line_sum_kernel(parts, qkv, out):
    total = jnp.sum(parts[...].astype(F32), axis=0)
    qkv[...] = total[:, 128:192]
    for x in range(4):
        out[x, 0:16, :] = total[:, 0:128]
        out[x, 16:32, :] = total[:, 256:384]


def finish_kernel(parts, proj, gain, table):
    low, high = [], []
    for x in range(4):
        proj[:, x * 128 : x * 128 + 128] = parts[x, 0:16, :]
        gain[:, x * 128 : x * 128 + 128] = parts[x, 24:25, :]
        low.append(parts[x, 16:20, :])
        high.append(parts[x, 20:24, :])
    pad = jnp.zeros((112, 128), F32)
    low = jnp.concatenate(low + [pad], axis=0)
    high = jnp.concatenate(high + [pad], axis=0)
    table[0:128, :] = low.T[:, 0:HEADS]
    table[128:NBIAS, :] = high.T[0 : NBIAS - 128, 0:HEADS]


def token_kernel(tok, cot, gain, own, above, left, diag, out, grads):
    for r in range(SHIFT):
        grads[r, 0:4, :] = diag[r].astype(F32)
        grads[r, 4:16, :] = above[r].astype(F32)
        grads[SHIFT + r, 0:4, :] = left[r].astype(F32)
        grads[SHIFT + r, 4:16, :] = own[r]
    hat, inv_std = layer_stats(tok[...].astype(F32))
    grad_hat = grads[...] * gain[...].reshape(1, 1, D)
    moved = (
        grad_hat
        - jnp.mean(grad_hat, axis=-1, keepdims=True)
        - hat * jnp.mean(grad_hat * hat, axis=-1, keepdims=True)
    )
    out[...] = (cot[...].astype(F32) + inv_std * moved).astype(BF16)


def shape(dims, dtype):
    return jax.ShapeDtypeStruct(dims, dtype)


def call(kernel, outs, args, scratch=(), flops=0, moved=0):
    return pl.pallas_call(
        kernel,
        out_shape=outs,
        scratch_shapes=list(scratch),
        compiler_params=ANY_PARAMS,
        cost_estimate=pl.CostEstimate(flops=flops, bytes_accessed=moved, transcendentals=0),
    )(*args)


def neighbour(value, down, right):
    pairs = [
        (r * NCOLS + c, ((r + down) % NROWS) * NCOLS + (c + right) % NCOLS)
        for r in range(NROWS)
        for c in range(NCOLS)
    ]
    return lax.ppermute(value, ROWS + COLS, pairs)


def local(tokens, cotangent, region, norm_gain, qkv_weight, out_weight, bias_table, bias_bucket):
    gain = norm_gain.reshape(1, D)
    to_up, to_left, to_diag = call(
        pack_kernel,
        [shape((9, 12, D), BF16), shape((9, 4, D), BF16), shape((9, 4, D), BF16)],
        (tokens, cotangent, region),
        moved=1 << 19,
    )
    up = neighbour(to_up, -1, 0)
    diag = neighbour(to_diag, -1, -1)
    left = neighbour(to_left, 0, -1)
    bias, bucket2 = call(
        bias_kernel,
        [shape((HEADS, AREA, 128), F32), shape((AREA, 128), jnp.int32)],
        (bias_table, bias_bucket),
        [pltpu.VMEM((256, 128), F32)],
        moved=1 << 23,
    )
    send, keep, own_grad, down_grad, right_grad, diag_grad = call(
        window_kernel,
        [
            shape((TOKENS + 16, 5 * D), BF16),
            shape((TOKENS, D), BF16),
            shape((4, 12, D), F32),
            shape((4, 12, D), BF16),
            shape((4, 4, D), BF16),
            shape((4, 4, D), BF16),
        ],
        (tokens, cotangent, region, up, left, diag, gain, qkv_weight, out_weight, bias, bucket2),
        [
            pltpu.VMEM((TOKENS, D), F32),
            pltpu.VMEM((TOKENS, D), F32),
            pltpu.VMEM((8, 128), F32),
            pltpu.VMEM((TOKENS, 3 * D), BF16),
            pltpu.VMEM((TOKENS, D), BF16),
            pltpu.VMEM((TOKENS, D), BF16),
            pltpu.VMEM((HEADS, AREA, 128), F32),
            pltpu.VMEM((TOKENS, D), F32),
        ],
        flops=1 << 30,
        moved=1 << 23,
    )
    other = lax.ppermute(send, "core", [(0, 1), (1, 0)])
    above_grad = neighbour(down_grad, 1, 0)
    left_grad = neighbour(right_grad, 0, 1)
    corner_grad = neighbour(diag_grad, 1, 1)
    products = call(
        product_kernel,
        shape((8, 4, 32, 640), BF16),
        (send, other, keep),
        flops=1 << 29,
        moved=1 << 21,
    )
    planes = lax.all_to_all(products.reshape(32, 32, 640), ("y", "x"), 0, 0)
    chunks = call(plane_sum_kernel, shape((12, 16, 384), BF16), (planes,), moved=1 << 21)
    lines = lax.all_to_all(chunks, ("zh", "zl"), 0, 0)
    grad_qkv, finals = call(
        line_sum_kernel, [shape((16, 64), F32), shape((4, 32, 128), F32)], (lines,), moved=1 << 18
    )
    finals = lax.all_to_all(finals, "x", 0, 0)
    grad_out_weight, grad_gain, grad_bias_table = call(
        finish_kernel,
        [shape((16, D), F32), shape((1, D), F32), shape((NBIAS, HEADS), F32)],
        (finals,),
        moved=1 << 17,
    )
    grad_tokens = call(
        token_kernel,
        shape((8, 16, D), BF16),
        (tokens, cotangent, gain, own_grad, above_grad, left_grad, corner_grad),
        [pltpu.VMEM((8, 16, D), F32)],
        moved=1 << 20,
    )
    return (grad_tokens, grad_qkv, grad_out_weight, grad_gain.reshape(D), grad_bias_table)


def solution(mesh):
    parts = Mesh(mesh.devices.reshape([n for _, n in PARTS]), [name for name, _ in PARTS])
    return jax.shard_map(
        local,
        mesh=parts,
        in_specs=(P(ROWS, COLS, None), P(ROWS, COLS, None), P(ROWS, COLS), P(), P(), P(), P(), P()),
        out_specs=(P(ROWS, COLS, None), P(ROWS, COLS), P(ROWS, None), P(), P()),
        check_vma=False,
    )
```

```python
import jax
import jax.numpy as jnp
from jax import lax
from jax.experimental import pallas as pl
from jax.experimental.pallas import tpu as pltpu
from jax.sharding import Mesh
from jax.sharding import PartitionSpec as P

D = 512
HEADS = 16
HEAD_DIM = 32
WIN = 8
SHIFT = 4
NBIAS = 225
AREA = WIN * WIN
TOKENS = 128
GROUP = 4
SCALE = HEAD_DIM ** (-0.5)
EPSILON = 1e-05

F32 = jnp.float32
BF16 = jnp.bfloat16

PARTS = (("y", 8), ("zh", 2), ("core", 2), ("x", 4), ("zl", 6))
ROWS = ("y", "zh", "core")
COLS = ("x", "zl")
NROWS = 32
NCOLS = 24

ANY_PARAMS = pltpu.CompilerParams(vmem_limit_bytes=48 * 1024 * 1024)


def dot(a, b):
    return lax.dot_general(a, b, (((1,), (0,)), ((), ())), preferred_element_type=F32)


def dot_nt(a, b):
    return lax.dot_general(a, b, (((1,), (1,)), ((), ())), preferred_element_type=F32)


def dot_tn(a, b):
    return lax.dot_general(a, b, (((0,), (0,)), ((), ())), preferred_element_type=F32)


def iota(shape, dim):
    return lax.broadcasted_iota(jnp.int32, shape, dim)


def split_high_low(value):
    high = value.astype(BF16)
    low = (value - high.astype(F32)).astype(BF16)
    return high, low


def layer_stats(floats):
    average = jnp.mean(floats, axis=-1, keepdims=True)
    centred = floats - average
    variance = jnp.mean(centred * centred, axis=-1, keepdims=True)
    inv_std = lax.rsqrt(variance + EPSILON)
    return centred * inv_std, inv_std


def pack_kernel(tok, cot, reg, to_up, to_left, to_diag, tok_v, cot_v, reg_v, sem):
    copies = [
        pltpu.make_async_copy(src, dst, sem.at[k])
        for k, (src, dst) in enumerate(((tok, tok_v), (cot, cot_v), (reg, reg_v)))
    ]
    for copy in copies:
        copy.start()
    to_up[96:112] = jnp.zeros((16, D), BF16)
    to_left[8] = jnp.zeros((4, D), BF16)
    to_diag[8] = jnp.zeros((4, D), BF16)
    for copy in copies:
        copy.wait()
    for k, src in ((0, tok_v), (4, cot_v)):
        for r in range(0, SHIFT, 2):
            first = src[r].astype(F32)
            second = src[r + 1].astype(F32)
            at = (k + r) * 12
            to_up[at : at + 24] = jnp.concatenate([first[4:16], second[4:16]], axis=0).astype(BF16)
        for r in range(SHIFT):
            to_diag[k + r] = src[r].astype(F32)[0:4].astype(BF16)
            to_left[k + r] = src[SHIFT + r].astype(F32)[0:4].astype(BF16)
    classes = reg_v[...].astype(F32)
    to_up[96:104, 0:16] = classes.astype(BF16)
    to_diag[8, 0:4, 0:16] = classes[0:4].astype(BF16)
    to_left[8, 0:4, 0:16] = classes[4:8].astype(BF16)


def bias_kernel(table, bucket, wqkv, wout, bias, bucket2, wqkv_out, wout_out, sem):
    copies = [
        pltpu.make_async_copy(wqkv, wqkv_out, sem.at[0]),
        pltpu.make_async_copy(wout, wout_out, sem.at[1]),
    ]
    for copy in copies:
        copy.start()
    turned = jnp.concatenate([table[...], jnp.zeros((HEADS, 256 - NBIAS), F32)], axis=1)
    both = jnp.concatenate([bucket[...], bucket[...]], axis=1)
    bucket2[...] = both
    for block in range(AREA // 8):
        index = both[block * 8 : block * 8 + 8]
        upper = index >= 128
        within = jnp.bitwise_and(index, 127)
        for h in range(HEADS):
            first = jnp.broadcast_to(turned[h : h + 1, 0:128], (8, 128))
            second = jnp.broadcast_to(turned[h : h + 1, 128:256], (8, 128))
            got_first = jnp.take_along_axis(first, within, axis=1, mode="promise_in_bounds")
            got_second = jnp.take_along_axis(second, within, axis=1, mode="promise_in_bounds")
            bias[h, block * 8 : block * 8 + 8, :] = jnp.where(upper, got_second, got_first)
    for copy in copies:
        copy.wait()


def window_kernel(
    tok, cot, reg, up, left, diag, gain, wqkv, wout, bias, bucket2,
    send, keep, own_grad, down_grad, right_grad, diag_grad,
    frame_t, frame_c, labels, packed, attended, grad_att, pairs, grad_in,
):
    up_f = up[...].astype(F32)
    for src, k, frame in ((tok, 0, frame_t), (cot, 4, frame_c)):
        for r in range(SHIFT):
            own = src[SHIFT + r].astype(F32)
            frame[r * 8 : r * 8 + 8, :] = own[4:12]
            frame[64 + r * 8 : 64 + r * 8 + 4, :] = own[12:16]
            frame[64 + r * 8 + 4 : 64 + r * 8 + 8, :] = left[k + r].astype(F32)
            s = SHIFT + r
            below = up_f[(k + r) * 12 : (k + r) * 12 + 12]
            frame[s * 8 : s * 8 + 8, :] = below[0:8]
            frame[64 + s * 8 : 64 + s * 8 + 4, :] = below[8:12]
            frame[64 + s * 8 + 4 : 64 + s * 8 + 8, :] = diag[k + r].astype(F32)

    mine = reg[...].astype(F32)
    labels[...] = jnp.zeros_like(labels)
    labels[0:4, 0:12] = mine[4:8, 4:16]
    labels[0:4, 12:16] = left[8, 0:4, 0:16].astype(F32)[:, 0:4]
    labels[4:8, 0:12] = up_f[96:100, 4:16]
    labels[4:8, 12:16] = diag[8, 0:4, 0:16].astype(F32)[:, 0:4]
    row_tile = (lax.axis_index("y") * 2 + lax.axis_index("zh")) * 2 + lax.axis_index("core")
    last = (row_tile == NROWS - 1).astype(F32)
    flags = jnp.where(iota((8, 128), 0) >= 4, 2.0, 0.0) * last
    coded = labels[...] + flags + jnp.where(iota((8, 128), 1) >= 8, 4.0, 0.0)
    token_lane = iota((128, 128), 1)
    token_row = iota((128, 128), 0)

    def column_of(token):
        return (token // 64) * 8 + token % 8

    def row_of(token):
        return (token // 8) % 8

    pick_lane = (column_of(token_lane) == token_row).astype(BF16)
    wide = dot(coded.astype(BF16), pick_lane)
    code_row = jnp.sum(
        jnp.where(row_of(iota((8, 128), 1)) == iota((8, 128), 0), wide, 0.0), axis=0, keepdims=True
    )
    pick_row = (column_of(token_row) == token_lane).astype(BF16)
    padded_codes = jnp.concatenate([coded, jnp.zeros((120, 128), F32)], axis=0).astype(BF16)
    tall = dot_nt(pick_row, padded_codes)
    code_col = jnp.sum(
        jnp.where(row_of(token_row) == token_lane, tall, 0.0), axis=1, keepdims=True
    )
    allowed = jnp.broadcast_to(code_col, (128, 128)) == jnp.broadcast_to(code_row, (128, 128))
    allowed4 = jnp.concatenate([allowed.astype(F32)] * GROUP, axis=0) > 0.5

    hat, _ = layer_stats(frame_t[...])
    normed = (hat * gain[...]).astype(BF16)
    cots = frame_c[...].astype(BF16)
    packed[...] = dot(normed, wqkv[...]).astype(BF16)
    grad_att[...] = dot_nt(cots, wout[...]).astype(BF16)
    send[0:TOKENS, 3 * D : 4 * D] = cots

    lane_head = iota((TOKENS, 128), 1) // HEAD_DIM
    masks = [lane_head == h for h in range(GROUP)]

    def stacked(value):
        return jnp.concatenate(
            [jnp.where(m, value, jnp.zeros_like(value)) for m in masks], axis=0
        )

    def beside(value):
        return jnp.concatenate([value[h * 128 : h * 128 + 128] for h in range(GROUP)], axis=1)

    for g in range(HEADS // GROUP):
        at = g * 128
        query = packed[:, at : at + 128]
        key = packed[:, D + at : D + at + 128]
        value = packed[:, 2 * D + at : 2 * D + at + 128]
        outer = grad_att[:, at : at + 128]
        query_s = stacked(query)
        outer_s = stacked(outer)
        biases = []
        for h in range(GROUP):
            one = bias[g * GROUP + h]
            biases += [one, one]
        scores = dot_nt(query_s, key) * SCALE + jnp.concatenate(biases, axis=0)
        scores = jnp.where(allowed4, scores, -1e30)
        raised = jnp.exp(scores - jnp.max(scores, axis=-1, keepdims=True))
        probs = raised / jnp.sum(raised, axis=-1, keepdims=True)
        probs_low = probs.astype(BF16)
        grad_probs = dot_nt(outer_s, value)
        inner = probs * grad_probs
        grad_scores = probs * (grad_probs - jnp.sum(inner, axis=-1, keepdims=True))
        grad_scaled = (grad_scores * SCALE).astype(BF16)
        attended[:, at : at + 128] = dot(beside(probs_low), stacked(value)).astype(BF16)
        send[0:TOKENS, at : at + 128] = dot(beside(grad_scaled), stacked(key)).astype(BF16)
        send[0:TOKENS, D + at : D + at + 128] = dot_tn(grad_scaled, query_s).astype(BF16)
        send[0:TOKENS, 2 * D + at : 2 * D + at + 128] = dot_tn(probs_low, outer_s).astype(BF16)
        for h in range(GROUP):
            one = grad_scores[h * 128 : h * 128 + 128]
            pairs[g * GROUP + h] = one[0:64] + one[64:128]

    core = lax.axis_index("core")
    for k, matrix in ((0, normed), (1, attended[...])):
        turned = matrix.astype(F32).T.reshape(16, 2, 16, TOKENS)
        even, odd = turned[:, 0].reshape(256, TOKENS), turned[:, 1].reshape(256, TOKENS)
        kept = jnp.where(core == 0, even, odd).astype(BF16)
        sent = jnp.where(core == 0, odd, even).astype(BF16)
        for b in range(2):
            lane = (2 * k + b) * 128
            keep[:, lane : lane + 128] = kept[b * 128 : b * 128 + 128]
            send[0:TOKENS, 4 * D + lane : 4 * D + lane + 128] = sent[b * 128 : b * 128 + 128]

    grad_normed = dot_nt(send[0:TOKENS, 0 : 3 * D], wqkv[...])
    grad_in[...] = grad_normed
    gain_sum = jnp.sum(grad_normed * hat, axis=0, keepdims=True)

    bucket_of = iota((256, 128), 0)

    def add_row(i, total):
        high, low = split_high_low(pairs[:, i, :])
        hot = (bucket_of == jnp.broadcast_to(bucket2[pl.ds(i, 1), :], (256, 128))).astype(BF16)
        return total + dot_nt(jnp.concatenate([high, low], axis=0), hot)

    sums = lax.fori_loop(0, AREA, add_row, jnp.zeros((2 * HEADS, 256), F32), unroll=8)
    table = sums[0:HEADS] + sums[HEADS : 2 * HEADS]
    high, low = split_high_low(table)
    send[TOKENS : TOKENS + 16, 0:256] = high
    send[TOKENS : TOKENS + 16, 256:512] = low
    high, low = split_high_low(jnp.concatenate([gain_sum, jnp.zeros((15, D), F32)], axis=0))
    send[TOKENS : TOKENS + 16, 512:1024] = high
    send[TOKENS : TOKENS + 16, 1024:1536] = low
    send[TOKENS : TOKENS + 16, 1536:2560] = jnp.zeros((16, 1024), BF16)

    for r in range(SHIFT):
        s = SHIFT + r
        own_grad[r, 0:8, :] = grad_in[r * 8 : r * 8 + 8, :]
        own_grad[r, 8:12, :] = grad_in[64 + r * 8 : 64 + r * 8 + 4, :]
        right_grad[r] = grad_in[64 + r * 8 : 64 + r * 8 + 8, :][4:8].astype(BF16)
        down_grad[r] = jnp.concatenate(
            [grad_in[s * 8 : s * 8 + 8, :], grad_in[64 + s * 8 : 64 + s * 8 + 8, :][0:4]], axis=0
        ).astype(BF16)
        diag_grad[r] = grad_in[64 + s * 8 : 64 + s * 8 + 8, :][4:8].astype(BF16)


def product_kernel(mine, other, keep, out):
    def rows(block):
        lane = block * 128
        return jnp.concatenate(
            [keep[:, lane : lane + 128], other[0:TOKENS, 4 * D + lane : 4 * D + lane + 128]], axis=1
        )

    right = jnp.concatenate([mine[0:TOKENS, 0 : 4 * D], other[0:TOKENS, 0 : 4 * D]], axis=0)
    for half in range(2):
        at = half * 128
        qkv = dot(rows(half), right[:, 0 : 3 * D]).astype(BF16)
        proj = dot(rows(2 + half), right[:, 3 * D : 4 * D]).astype(BF16)
        for x in range(4):
            out[x, at : at + 128, 0:384] = qkv[:, x * 384 : x * 384 + 384]
            out[x, at : at + 128, 384:512] = proj[:, x * 128 : x * 128 + 128]
    small = mine[TOKENS : TOKENS + 16, 0:1536].astype(F32) + other[TOKENS : TOKENS + 16, 0:1536].astype(F32)
    table = small[:, 0:256] + small[:, 256:512]
    gain = small[0:8, 512:1024] + small[0:8, 1024:1536]
    for x in range(4):
        part = jnp.concatenate(
            [
                table[4 * x : 4 * x + 4, 0:128],
                table[4 * x : 4 * x + 4, 128:256],
                gain[:, x * 128 : x * 128 + 128],
            ],
            axis=0,
        )
        high, low = split_high_low(part)
        out[x, 256:272, 0:128] = high
        out[x, 256:272, 128:256] = low
        out[x, 256:272, 256:512] = jnp.zeros((16, 256), BF16)


def across_sum_kernel(parts, out):
    small = jnp.sum(parts[:, 256:272, 0:256].astype(F32), axis=0)
    high, low = split_high_low(small[:, 0:128] + small[:, 128:256])
    both = jnp.concatenate([high, low], axis=0)
    for y in range(8):
        total = jnp.sum(parts[:, y * 32 : y * 32 + 32, :].astype(F32), axis=0)
        out[y, :, 0:512] = total.astype(BF16)
        out[y, :, 512:640] = both


def plane_sum_kernel(parts, out):
    total = jnp.sum(parts[...].astype(F32), axis=0)
    small = (total[0:16, 512:640] + total[16:32, 512:640]).astype(BF16)
    for zh in range(2):
        rows = total[zh * 16 : zh * 16 + 16]
        proj = rows[:, 384:512].astype(BF16)
        for zl in range(6):
            lane = (zl // 2) * 128
            qkv = rows[:, lane : lane + 128]
            if zl % 2 == 1:
                qkv = pltpu.roll(qkv, 64, 1)
            out[zh * 6 + zl, :, 0:128] = proj
            out[zh * 6 + zl, :, 128:256] = qkv.astype(BF16)
            out[zh * 6 + zl, :, 256:384] = small


def line_sum_kernel(parts, qkv, out):
    total = jnp.sum(parts[...].astype(F32), axis=0)
    qkv[...] = total[:, 128:192]
    for x in range(4):
        out[x, 0:16, :] = total[:, 0:128]
        out[x, 16:32, :] = total[:, 256:384]


def finish_kernel(parts, proj, gain, table):
    low, high = [], []
    for x in range(4):
        proj[:, x * 128 : x * 128 + 128] = parts[x, 0:16, :]
        gain[:, x * 128 : x * 128 + 128] = parts[x, 24:25, :]
        low.append(parts[x, 16:20, :])
        high.append(parts[x, 20:24, :])
    table[:, 0:128] = jnp.concatenate(low, axis=0)
    table[:, 128:NBIAS] = jnp.concatenate(high, axis=0)[:, 0 : NBIAS - 128]


def token_kernel(tok, cot, gain, own, above, left, diag, out, grads):
    for r in range(SHIFT):
        grads[r, 0:4, :] = diag[r].astype(F32)
        grads[r, 4:16, :] = above[r].astype(F32)
        grads[SHIFT + r, 0:4, :] = left[r].astype(F32)
        grads[SHIFT + r, 4:16, :] = own[r]
    hat, inv_std = layer_stats(tok[...].astype(F32))
    grad_hat = grads[...] * gain[...].reshape(1, 1, D)
    moved = (
        grad_hat
        - jnp.mean(grad_hat, axis=-1, keepdims=True)
        - hat * jnp.mean(grad_hat * hat, axis=-1, keepdims=True)
    )
    out[...] = (cot[...].astype(F32) + inv_std * moved).astype(BF16)


def shape(dims, dtype):
    return jax.ShapeDtypeStruct(dims, dtype)


def call(kernel, outs, args, scratch=(), flops=0, moved=0, remain=(), params=ANY_PARAMS):
    return pl.pallas_call(
        kernel,
        in_specs=[
            pl.BlockSpec(memory_space=pltpu.HBM if k in remain else pltpu.VMEM)
            for k in range(len(args))
        ],
        out_shape=outs,
        scratch_shapes=list(scratch),
        compiler_params=params,
        cost_estimate=pl.CostEstimate(flops=flops, bytes_accessed=moved, transcendentals=0),
    )(*args)


def neighbour(value, down, right):
    pairs = [
        (r * NCOLS + c, ((r + down) % NROWS) * NCOLS + (c + right) % NCOLS)
        for r in range(NROWS)
        for c in range(NCOLS)
    ]
    return lax.ppermute(value, ROWS + COLS, pairs)


def local(tokens, cotangent, region, norm_gain, qkv_weight, out_weight, bias_table, bias_bucket):
    gain = norm_gain.reshape(1, D)
    to_up, to_left, to_diag = call(
        pack_kernel,
        [shape((112, D), BF16), shape((9, 4, D), BF16), shape((9, 4, D), BF16)],
        (tokens, cotangent, region),
        [
            pltpu.VMEM((8, 16, D), BF16),
            pltpu.VMEM((8, 16, D), BF16),
            pltpu.VMEM((8, 16), jnp.int32),
            pltpu.SemaphoreType.DMA((3,)),
        ],
        moved=1 << 19,
        remain=(0, 1, 2),
        params=pltpu.CompilerParams(),
    )
    up = neighbour(to_up, -1, 0)
    diag = neighbour(to_diag, -1, -1)
    left = neighbour(to_left, 0, -1)
    bias, bucket2, wqkv, wout = call(
        bias_kernel,
        [
            shape((HEADS, AREA, 128), F32),
            shape((AREA, 128), jnp.int32),
            shape((D, 3 * D), BF16),
            shape((D, D), BF16),
        ],
        (bias_table.T, bias_bucket, qkv_weight, out_weight),
        [pltpu.SemaphoreType.DMA((2,))],
        moved=1 << 23,
        remain=(2, 3),
    )
    send, keep, own_grad, down_grad, right_grad, diag_grad = call(
        window_kernel,
        [
            shape((TOKENS + 16, 5 * D), BF16),
            shape((TOKENS, D), BF16),
            shape((4, 12, D), F32),
            shape((4, 12, D), BF16),
            shape((4, 4, D), BF16),
            shape((4, 4, D), BF16),
        ],
        (tokens, cotangent, region, up, left, diag, gain, wqkv, wout, bias, bucket2),
        [
            pltpu.VMEM((TOKENS, D), F32),
            pltpu.VMEM((TOKENS, D), F32),
            pltpu.VMEM((8, 128), F32),
            pltpu.VMEM((TOKENS, 3 * D), BF16),
            pltpu.VMEM((TOKENS, D), BF16),
            pltpu.VMEM((TOKENS, D), BF16),
            pltpu.VMEM((HEADS, AREA, 128), F32),
            pltpu.VMEM((TOKENS, D), F32),
        ],
        flops=1 << 30,
        moved=1 << 23,
    )
    other = lax.ppermute(send, "core", [(0, 1), (1, 0)])
    products = call(
        product_kernel,
        shape((4, 272, D), BF16),
        (send, other, keep),
        flops=1 << 29,
        moved=1 << 21,
    )
    across = lax.all_to_all(products, "x", 0, 0)
    halves = call(across_sum_kernel, shape((8, 32, 640), BF16), (across,), moved=1 << 21)
    planes = lax.all_to_all(halves, "y", 0, 0)
    chunks = call(plane_sum_kernel, shape((12, 16, 384), BF16), (planes,), moved=1 << 21)
    chunks, down_grad, right_grad, diag_grad = lax.optimization_barrier(
        (chunks, down_grad, right_grad, diag_grad)
    )
    lines = lax.all_to_all(chunks, ("zh", "zl"), 0, 0)
    above_grad = neighbour(down_grad, 1, 0)
    left_grad = neighbour(right_grad, 0, 1)
    corner_grad = neighbour(diag_grad, 1, 1)
    grad_qkv, finals = call(
        line_sum_kernel, [shape((16, 64), F32), shape((4, 32, 128), F32)], (lines,), moved=1 << 18
    )
    finals, above_grad, left_grad, corner_grad = lax.optimization_barrier(
        (finals, above_grad, left_grad, corner_grad)
    )
    finals = lax.all_to_all(finals, "x", 0, 0)
    grad_tokens = call(
        token_kernel,
        shape((8, 16, D), BF16),
        (tokens, cotangent, gain, own_grad, above_grad, left_grad, corner_grad),
        [pltpu.VMEM((8, 16, D), F32)],
        moved=1 << 20,
    )
    grad_out_weight, grad_gain, grad_bias_table = call(
        finish_kernel,
        [shape((16, D), F32), shape((1, D), F32), shape((HEADS, NBIAS), F32)],
        (finals,),
        moved=1 << 17,
    )
    return (grad_tokens, grad_qkv, grad_out_weight, grad_gain.reshape(D), grad_bias_table.T)


def solution(mesh):
    parts = Mesh(mesh.devices.reshape([n for _, n in PARTS]), [name for name, _ in PARTS])
    return jax.shard_map(
        local,
        mesh=parts,
        in_specs=(P(ROWS, COLS, None), P(ROWS, COLS, None), P(ROWS, COLS), P(), P(), P(), P(), P()),
        out_specs=(P(ROWS, COLS, None), P(ROWS, COLS), P(ROWS, None), P(), P()),
        check_vma=False,
    )
```

```python
import jax
import jax.numpy as jnp
from jax import lax
from jax.experimental import pallas as pl
from jax.experimental.pallas import tpu as pltpu
from jax.sharding import Mesh
from jax.sharding import PartitionSpec as P

D = 512
HEADS = 16
HEAD_DIM = 32
WIN = 8
SHIFT = 4
NBIAS = 225
AREA = WIN * WIN
TOKENS = 128
GROUP = 4
SCALE = HEAD_DIM ** (-0.5)
EPSILON = 1e-05

F32 = jnp.float32
BF16 = jnp.bfloat16

PARTS = (("y", 8), ("zh", 2), ("core", 2), ("x", 4), ("zl", 6))
ROWS = ("y", "zh", "core")
COLS = ("x", "zl")
NROWS = 32
NCOLS = 24

ANY_PARAMS = pltpu.CompilerParams(vmem_limit_bytes=48 * 1024 * 1024)


def dot(a, b):
    return lax.dot_general(a, b, (((1,), (0,)), ((), ())), preferred_element_type=F32)


def dot_nt(a, b):
    return lax.dot_general(a, b, (((1,), (1,)), ((), ())), preferred_element_type=F32)


def dot_tn(a, b):
    return lax.dot_general(a, b, (((0,), (0,)), ((), ())), preferred_element_type=F32)


def iota(shape, dim):
    return lax.broadcasted_iota(jnp.int32, shape, dim)


def split_high_low(value):
    high = value.astype(BF16)
    low = (value - high.astype(F32)).astype(BF16)
    return high, low


def layer_stats(floats):
    average = jnp.mean(floats, axis=-1, keepdims=True)
    centred = floats - average
    variance = jnp.mean(centred * centred, axis=-1, keepdims=True)
    inv_std = lax.rsqrt(variance + EPSILON)
    return centred * inv_std, inv_std


def pack_kernel(tok, cot, reg, to_up, to_left, to_diag, tok_v, cot_v, reg_v, sem):
    copies = [
        pltpu.make_async_copy(src, dst, sem.at[k])
        for k, (src, dst) in enumerate(((tok, tok_v), (cot, cot_v), (reg, reg_v)))
    ]
    for copy in copies:
        copy.start()
    to_up[96:112] = jnp.zeros((16, D), BF16)
    to_left[8] = jnp.zeros((4, D), BF16)
    to_diag[8] = jnp.zeros((4, D), BF16)
    for copy in copies:
        copy.wait()
    for k, src in ((0, tok_v), (4, cot_v)):
        for r in range(0, SHIFT, 2):
            first = src[r].astype(F32)
            second = src[r + 1].astype(F32)
            at = (k + r) * 12
            to_up[at : at + 24] = jnp.concatenate([first[4:16], second[4:16]], axis=0).astype(BF16)
        for r in range(SHIFT):
            to_diag[k + r] = src[r].astype(F32)[0:4].astype(BF16)
            to_left[k + r] = src[SHIFT + r].astype(F32)[0:4].astype(BF16)
    classes = reg_v[...].astype(F32)
    to_up[96:104, 0:16] = classes.astype(BF16)
    to_diag[8, 0:4, 0:16] = classes[0:4].astype(BF16)
    to_left[8, 0:4, 0:16] = classes[4:8].astype(BF16)


def bias_kernel(table_far, bucket_far, bias, bucket2, table, bucket, sem):
    copies = [
        pltpu.make_async_copy(table_far, table, sem.at[0]),
        pltpu.make_async_copy(bucket_far, bucket, sem.at[1]),
    ]
    for copy in copies:
        copy.start()
    for copy in copies:
        copy.wait()
    turned = jnp.concatenate([table[...], jnp.zeros((HEADS, 256 - NBIAS), F32)], axis=1)
    both = jnp.concatenate([bucket[...], bucket[...]], axis=1)
    bucket2[...] = both
    for block in range(AREA // 8):
        index = both[block * 8 : block * 8 + 8]
        upper = index >= 128
        within = jnp.bitwise_and(index, 127)
        for h in range(HEADS):
            first = jnp.broadcast_to(turned[h : h + 1, 0:128], (8, 128))
            second = jnp.broadcast_to(turned[h : h + 1, 128:256], (8, 128))
            got_first = jnp.take_along_axis(first, within, axis=1, mode="promise_in_bounds")
            got_second = jnp.take_along_axis(second, within, axis=1, mode="promise_in_bounds")
            bias[h, block * 8 : block * 8 + 8, :] = jnp.where(upper, got_second, got_first)


def window_kernel(
    tok_far, cot_far, reg_far, wqkv_far, wout_far, gain_far, bias, bucket2, up, left, diag,
    send, keep, own_grad, down_grad, right_grad, diag_grad,
    frame_t, frame_c, labels, packed, attended, grad_att, pairs, grad_in,
    tok, cot, reg, wqkv, wout, gain, sem,
):
    moves = (
        (tok_far, tok), (cot_far, cot), (reg_far, reg), (wqkv_far, wqkv),
        (wout_far, wout), (gain_far, gain),
    )
    copies = [pltpu.make_async_copy(src, dst, sem.at[k]) for k, (src, dst) in enumerate(moves)]
    for copy in copies:
        copy.start()
    for copy in copies[0:3]:
        copy.wait()

    up_f = up[...].astype(F32)
    for src, k, frame in ((tok, 0, frame_t), (cot, 4, frame_c)):
        for r in range(SHIFT):
            own = src[SHIFT + r].astype(F32)
            frame[r * 8 : r * 8 + 8, :] = own[4:12]
            frame[64 + r * 8 : 64 + r * 8 + 4, :] = own[12:16]
            frame[64 + r * 8 + 4 : 64 + r * 8 + 8, :] = left[k + r].astype(F32)
            s = SHIFT + r
            below = up_f[(k + r) * 12 : (k + r) * 12 + 12]
            frame[s * 8 : s * 8 + 8, :] = below[0:8]
            frame[64 + s * 8 : 64 + s * 8 + 4, :] = below[8:12]
            frame[64 + s * 8 + 4 : 64 + s * 8 + 8, :] = diag[k + r].astype(F32)

    mine = reg[...].astype(F32)
    labels[...] = jnp.zeros_like(labels)
    labels[0:4, 0:12] = mine[4:8, 4:16]
    labels[0:4, 12:16] = left[8, 0:4, 0:16].astype(F32)[:, 0:4]
    labels[4:8, 0:12] = up_f[96:100, 4:16]
    labels[4:8, 12:16] = diag[8, 0:4, 0:16].astype(F32)[:, 0:4]
    row_tile = (lax.axis_index("y") * 2 + lax.axis_index("zh")) * 2 + lax.axis_index("core")
    last = (row_tile == NROWS - 1).astype(F32)
    flags = jnp.where(iota((8, 128), 0) >= 4, 2.0, 0.0) * last
    coded = labels[...] + flags + jnp.where(iota((8, 128), 1) >= 8, 4.0, 0.0)
    token_lane = iota((128, 128), 1)
    token_row = iota((128, 128), 0)

    def column_of(token):
        return (token // 64) * 8 + token % 8

    def row_of(token):
        return (token // 8) % 8

    pick_lane = (column_of(token_lane) == token_row).astype(BF16)
    wide = dot(coded.astype(BF16), pick_lane)
    code_row = jnp.sum(
        jnp.where(row_of(iota((8, 128), 1)) == iota((8, 128), 0), wide, 0.0), axis=0, keepdims=True
    )
    pick_row = (column_of(token_row) == token_lane).astype(BF16)
    padded_codes = jnp.concatenate([coded, jnp.zeros((120, 128), F32)], axis=0).astype(BF16)
    tall = dot_nt(pick_row, padded_codes)
    code_col = jnp.sum(
        jnp.where(row_of(token_row) == token_lane, tall, 0.0), axis=1, keepdims=True
    )
    allowed = jnp.broadcast_to(code_col, (128, 128)) == jnp.broadcast_to(code_row, (128, 128))
    allowed4 = jnp.concatenate([allowed.astype(F32)] * GROUP, axis=0) > 0.5

    hat, _ = layer_stats(frame_t[...])
    copies[5].wait()
    normed = (hat * gain[...]).astype(BF16)
    cots = frame_c[...].astype(BF16)
    for copy in copies[3:5]:
        copy.wait()
    packed[...] = dot(normed, wqkv[...]).astype(BF16)
    grad_att[...] = dot_nt(cots, wout[...]).astype(BF16)
    send[0:TOKENS, 3 * D : 4 * D] = cots

    lane_head = iota((TOKENS, 128), 1) // HEAD_DIM
    masks = [lane_head == h for h in range(GROUP)]

    def stacked(value):
        return jnp.concatenate(
            [jnp.where(m, value, jnp.zeros_like(value)) for m in masks], axis=0
        )

    def beside(value):
        return jnp.concatenate([value[h * 128 : h * 128 + 128] for h in range(GROUP)], axis=1)

    for g in range(HEADS // GROUP):
        at = g * 128
        query = packed[:, at : at + 128]
        key = packed[:, D + at : D + at + 128]
        value = packed[:, 2 * D + at : 2 * D + at + 128]
        outer = grad_att[:, at : at + 128]
        query_s = stacked(query)
        outer_s = stacked(outer)
        biases = []
        for h in range(GROUP):
            one = bias[g * GROUP + h]
            biases += [one, one]
        scores = dot_nt(query_s, key) * SCALE + jnp.concatenate(biases, axis=0)
        scores = jnp.where(allowed4, scores, -1e30)
        raised = jnp.exp(scores - jnp.max(scores, axis=-1, keepdims=True))
        probs = raised / jnp.sum(raised, axis=-1, keepdims=True)
        probs_low = probs.astype(BF16)
        grad_probs = dot_nt(outer_s, value)
        inner = probs * grad_probs
        grad_scores = probs * (grad_probs - jnp.sum(inner, axis=-1, keepdims=True))
        grad_scaled = (grad_scores * SCALE).astype(BF16)
        attended[:, at : at + 128] = dot(beside(probs_low), stacked(value)).astype(BF16)
        send[0:TOKENS, at : at + 128] = dot(beside(grad_scaled), stacked(key)).astype(BF16)
        send[0:TOKENS, D + at : D + at + 128] = dot_tn(grad_scaled, query_s).astype(BF16)
        send[0:TOKENS, 2 * D + at : 2 * D + at + 128] = dot_tn(probs_low, outer_s).astype(BF16)
        for h in range(GROUP):
            one = grad_scores[h * 128 : h * 128 + 128]
            pairs[g * GROUP + h] = one[0:64] + one[64:128]

    core = lax.axis_index("core")
    for k, matrix in ((0, normed), (1, attended[...])):
        turned = matrix.astype(F32).T.reshape(16, 2, 16, TOKENS)
        even, odd = turned[:, 0].reshape(256, TOKENS), turned[:, 1].reshape(256, TOKENS)
        kept = jnp.where(core == 0, even, odd).astype(BF16)
        sent = jnp.where(core == 0, odd, even).astype(BF16)
        for b in range(2):
            lane = (2 * k + b) * 128
            keep[:, lane : lane + 128] = kept[b * 128 : b * 128 + 128]
            send[0:TOKENS, 4 * D + lane : 4 * D + lane + 128] = sent[b * 128 : b * 128 + 128]

    grad_normed = dot_nt(send[0:TOKENS, 0 : 3 * D], wqkv[...])
    grad_in[...] = grad_normed
    gain_sum = jnp.sum(grad_normed * hat, axis=0, keepdims=True)

    bucket_of = iota((256, 128), 0)

    def add_row(i, total):
        high, low = split_high_low(pairs[:, i, :])
        hot = (bucket_of == jnp.broadcast_to(bucket2[pl.ds(i, 1), :], (256, 128))).astype(BF16)
        return total + dot_nt(jnp.concatenate([high, low], axis=0), hot)

    sums = lax.fori_loop(0, AREA, add_row, jnp.zeros((2 * HEADS, 256), F32), unroll=8)
    table = sums[0:HEADS] + sums[HEADS : 2 * HEADS]
    high, low = split_high_low(table)
    send[TOKENS : TOKENS + 16, 0:256] = high
    send[TOKENS : TOKENS + 16, 256:512] = low
    high, low = split_high_low(jnp.concatenate([gain_sum, jnp.zeros((15, D), F32)], axis=0))
    send[TOKENS : TOKENS + 16, 512:1024] = high
    send[TOKENS : TOKENS + 16, 1024:1536] = low
    send[TOKENS : TOKENS + 16, 1536:2560] = jnp.zeros((16, 1024), BF16)

    for r in range(SHIFT):
        s = SHIFT + r
        own_grad[r, 0:8, :] = grad_in[r * 8 : r * 8 + 8, :]
        own_grad[r, 8:12, :] = grad_in[64 + r * 8 : 64 + r * 8 + 4, :]
        right_grad[r] = grad_in[64 + r * 8 : 64 + r * 8 + 8, :][4:8].astype(BF16)
        down_grad[r] = jnp.concatenate(
            [grad_in[s * 8 : s * 8 + 8, :], grad_in[64 + s * 8 : 64 + s * 8 + 8, :][0:4]], axis=0
        ).astype(BF16)
        diag_grad[r] = grad_in[64 + s * 8 : 64 + s * 8 + 8, :][4:8].astype(BF16)


def product_kernel(mine, other, keep, out):
    def rows(block):
        lane = block * 128
        return jnp.concatenate(
            [keep[:, lane : lane + 128], other[0:TOKENS, 4 * D + lane : 4 * D + lane + 128]], axis=1
        )

    right = jnp.concatenate([mine[0:TOKENS, 0 : 4 * D], other[0:TOKENS, 0 : 4 * D]], axis=0)
    for half in range(2):
        at = half * 128
        qkv = dot(rows(half), right[:, 0 : 3 * D]).astype(BF16)
        proj = dot(rows(2 + half), right[:, 3 * D : 4 * D]).astype(BF16)
        for x in range(4):
            out[x, at : at + 128, 0:384] = qkv[:, x * 384 : x * 384 + 384]
            out[x, at : at + 128, 384:512] = proj[:, x * 128 : x * 128 + 128]
    small = mine[TOKENS : TOKENS + 16, 0:1536].astype(F32) + other[TOKENS : TOKENS + 16, 0:1536].astype(F32)
    table = small[:, 0:256] + small[:, 256:512]
    gain = small[0:8, 512:1024] + small[0:8, 1024:1536]
    for x in range(4):
        part = jnp.concatenate(
            [
                table[4 * x : 4 * x + 4, 0:128],
                table[4 * x : 4 * x + 4, 128:256],
                gain[:, x * 128 : x * 128 + 128],
            ],
            axis=0,
        )
        high, low = split_high_low(part)
        out[x, 256:272, 0:128] = high
        out[x, 256:272, 128:256] = low
        out[x, 256:272, 256:512] = jnp.zeros((16, 256), BF16)


def across_sum_kernel(parts, out):
    small = jnp.sum(parts[:, 256:272, 0:256].astype(F32), axis=0)
    high, low = split_high_low(small[:, 0:128] + small[:, 128:256])
    both = jnp.concatenate([high, low], axis=0)
    for y in range(8):
        total = jnp.sum(parts[:, y * 32 : y * 32 + 32, :].astype(F32), axis=0)
        out[y, :, 0:512] = total.astype(BF16)
        out[y, :, 512:640] = both


def plane_sum_kernel(parts, out):
    total = jnp.sum(parts[...].astype(F32), axis=0)
    small = (total[0:16, 512:640] + total[16:32, 512:640]).astype(BF16)
    for zh in range(2):
        rows = total[zh * 16 : zh * 16 + 16]
        proj = rows[:, 384:512].astype(BF16)
        for zl in range(6):
            lane = (zl // 2) * 128
            qkv = rows[:, lane : lane + 128]
            if zl % 2 == 1:
                qkv = pltpu.roll(qkv, 64, 1)
            out[zh * 6 + zl, :, 0:128] = proj
            out[zh * 6 + zl, :, 128:256] = qkv.astype(BF16)
            out[zh * 6 + zl, :, 256:384] = small


def line_sum_kernel(parts, qkv, out):
    total = jnp.sum(parts[...].astype(F32), axis=0)
    qkv[...] = total[:, 128:192]
    for x in range(4):
        out[x, 0:16, :] = total[:, 0:128]
        out[x, 16:32, :] = total[:, 256:384]


def finish_kernel(parts, proj, gain, table):
    low, high = [], []
    for x in range(4):
        proj[:, x * 128 : x * 128 + 128] = parts[x, 0:16, :]
        gain[:, x * 128 : x * 128 + 128] = parts[x, 24:25, :]
        low.append(parts[x, 16:20, :])
        high.append(parts[x, 20:24, :])
    table[:, 0:128] = jnp.concatenate(low, axis=0)
    table[:, 128:NBIAS] = jnp.concatenate(high, axis=0)[:, 0 : NBIAS - 128]


def token_kernel(tok, cot, gain, own, above, left, diag, out, grads):
    for r in range(SHIFT):
        grads[r, 0:4, :] = diag[r].astype(F32)
        grads[r, 4:16, :] = above[r].astype(F32)
        grads[SHIFT + r, 0:4, :] = left[r].astype(F32)
        grads[SHIFT + r, 4:16, :] = own[r]
    hat, inv_std = layer_stats(tok[...].astype(F32))
    grad_hat = grads[...] * gain[...].reshape(1, 1, D)
    moved = (
        grad_hat
        - jnp.mean(grad_hat, axis=-1, keepdims=True)
        - hat * jnp.mean(grad_hat * hat, axis=-1, keepdims=True)
    )
    out[...] = (cot[...].astype(F32) + inv_std * moved).astype(BF16)


def shape(dims, dtype):
    return jax.ShapeDtypeStruct(dims, dtype)


def call(kernel, outs, args, scratch=(), flops=0, moved=0, remain=(), params=ANY_PARAMS):
    args = [
        pltpu.with_memory_space_constraint(arg, pltpu.HBM) if k in remain else arg
        for k, arg in enumerate(args)
    ]
    return pl.pallas_call(
        kernel,
        in_specs=[
            pl.BlockSpec(memory_space=pltpu.HBM if k in remain else pltpu.VMEM)
            for k in range(len(args))
        ],
        out_shape=outs,
        scratch_shapes=list(scratch),
        compiler_params=params,
        cost_estimate=pl.CostEstimate(flops=flops, bytes_accessed=moved, transcendentals=0),
    )(*args)


def neighbour(value, down, right):
    pairs = [
        (r * NCOLS + c, ((r + down) % NROWS) * NCOLS + (c + right) % NCOLS)
        for r in range(NROWS)
        for c in range(NCOLS)
    ]
    return lax.ppermute(value, ROWS + COLS, pairs)


def local(tokens, cotangent, region, norm_gain, qkv_weight, out_weight, bias_table, bias_bucket):
    gain = norm_gain.reshape(1, D)
    to_up, to_left, to_diag = call(
        pack_kernel,
        [shape((112, D), BF16), shape((9, 4, D), BF16), shape((9, 4, D), BF16)],
        (tokens, cotangent, region),
        [
            pltpu.VMEM((8, 16, D), BF16),
            pltpu.VMEM((8, 16, D), BF16),
            pltpu.VMEM((8, 16), jnp.int32),
            pltpu.SemaphoreType.DMA((3,)),
        ],
        moved=1 << 19,
        remain=(0, 1, 2),
    )
    up = neighbour(to_up, -1, 0)
    diag = neighbour(to_diag, -1, -1)
    left = neighbour(to_left, 0, -1)
    bias, bucket2 = call(
        bias_kernel,
        [
            shape((HEADS, AREA, 128), F32),
            shape((AREA, 128), jnp.int32),
        ],
        (bias_table.T, bias_bucket),
        [
            pltpu.VMEM((HEADS, NBIAS), F32),
            pltpu.VMEM((AREA, AREA), jnp.int32),
            pltpu.SemaphoreType.DMA((2,)),
        ],
        moved=1 << 23,
        remain=(0, 1),
    )
    send, keep, own_grad, down_grad, right_grad, diag_grad = call(
        window_kernel,
        [
            shape((TOKENS + 16, 5 * D), BF16),
            shape((TOKENS, D), BF16),
            shape((4, 12, D), F32),
            shape((4, 12, D), BF16),
            shape((4, 4, D), BF16),
            shape((4, 4, D), BF16),
        ],
        (tokens, cotangent, region, qkv_weight, out_weight, gain, bias, bucket2, up, left, diag),
        [
            pltpu.VMEM((TOKENS, D), F32),
            pltpu.VMEM((TOKENS, D), F32),
            pltpu.VMEM((8, 128), F32),
            pltpu.VMEM((TOKENS, 3 * D), BF16),
            pltpu.VMEM((TOKENS, D), BF16),
            pltpu.VMEM((TOKENS, D), BF16),
            pltpu.VMEM((HEADS, AREA, 128), F32),
            pltpu.VMEM((TOKENS, D), F32),
            pltpu.VMEM((8, 16, D), BF16),
            pltpu.VMEM((8, 16, D), BF16),
            pltpu.VMEM((8, 16), jnp.int32),
            pltpu.VMEM((D, 3 * D), BF16),
            pltpu.VMEM((D, D), BF16),
            pltpu.VMEM((1, D), F32),
            pltpu.SemaphoreType.DMA((6,)),
        ],
        flops=1 << 30,
        moved=1 << 23,
        remain=tuple(range(6)),
    )
    other = lax.ppermute(send, "core", [(0, 1), (1, 0)])
    products = call(
        product_kernel,
        shape((4, 272, D), BF16),
        (send, other, keep),
        flops=1 << 29,
        moved=1 << 21,
    )
    products, down_grad, right_grad, diag_grad = lax.optimization_barrier(
        (products, down_grad, right_grad, diag_grad)
    )
    across = lax.all_to_all(products, "x", 0, 0)
    above_grad = neighbour(down_grad, 1, 0)
    left_grad = neighbour(right_grad, 0, 1)
    corner_grad = neighbour(diag_grad, 1, 1)
    halves = call(across_sum_kernel, shape((8, 32, 640), BF16), (across,), moved=1 << 21)
    halves, above_grad, left_grad, corner_grad = lax.optimization_barrier(
        (halves, above_grad, left_grad, corner_grad)
    )
    planes = lax.all_to_all(halves, "y", 0, 0)
    chunks = call(plane_sum_kernel, shape((12, 16, 384), BF16), (planes,), moved=1 << 21)
    lines = lax.all_to_all(chunks, ("zh", "zl"), 0, 0)
    grad_qkv, finals = call(
        line_sum_kernel, [shape((16, 64), F32), shape((4, 32, 128), F32)], (lines,), moved=1 << 18
    )
    finals = lax.all_to_all(finals, "x", 0, 0)
    grad_tokens = call(
        token_kernel,
        shape((8, 16, D), BF16),
        (tokens, cotangent, gain, own_grad, above_grad, left_grad, corner_grad),
        [pltpu.VMEM((8, 16, D), F32)],
        moved=1 << 20,
    )
    grad_out_weight, grad_gain, grad_bias_table = call(
        finish_kernel,
        [shape((16, D), F32), shape((1, D), F32), shape((HEADS, NBIAS), F32)],
        (finals,),
        moved=1 << 17,
    )
    return (grad_tokens, grad_qkv, grad_out_weight, grad_gain.reshape(D), grad_bias_table.T)


def solution(mesh):
    parts = Mesh(mesh.devices.reshape([n for _, n in PARTS]), [name for name, _ in PARTS])
    return jax.shard_map(
        local,
        mesh=parts,
        in_specs=(P(ROWS, COLS, None), P(ROWS, COLS, None), P(ROWS, COLS), P(), P(), P(), P(), P()),
        out_specs=(P(ROWS, COLS, None), P(ROWS, COLS), P(ROWS, None), P(), P()),
        check_vma=False,
    )
```

```python
import jax
import jax.numpy as jnp
from jax import lax
from jax.experimental import pallas as pl
from jax.experimental.pallas import tpu as pltpu
from jax.sharding import Mesh
from jax.sharding import PartitionSpec as P

D = 512
HEADS = 16
HEAD_DIM = 32
WIN = 8
SHIFT = 4
NBIAS = 225
AREA = WIN * WIN
TOKENS = 128
GROUP = 4
SCALE = HEAD_DIM ** (-0.5)
EPSILON = 1e-05

F32 = jnp.float32
BF16 = jnp.bfloat16

PARTS = (("y", 8), ("zh", 2), ("core", 2), ("x", 4), ("zl", 6))
ROWS = ("y", "zh", "core")
COLS = ("x", "zl")
NROWS = 32
NCOLS = 24

ANY_PARAMS = pltpu.CompilerParams(vmem_limit_bytes=48 * 1024 * 1024)


def dot(a, b):
    return lax.dot_general(a, b, (((1,), (0,)), ((), ())), preferred_element_type=F32)


def dot_nt(a, b):
    return lax.dot_general(a, b, (((1,), (1,)), ((), ())), preferred_element_type=F32)


def dot_tn(a, b):
    return lax.dot_general(a, b, (((0,), (0,)), ((), ())), preferred_element_type=F32)


def iota(shape, dim):
    return lax.broadcasted_iota(jnp.int32, shape, dim)


def split_high_low(value):
    high = value.astype(BF16)
    low = (value - high.astype(F32)).astype(BF16)
    return high, low


def layer_stats(floats):
    average = jnp.mean(floats, axis=-1, keepdims=True)
    centred = floats - average
    variance = jnp.mean(centred * centred, axis=-1, keepdims=True)
    inv_std = lax.rsqrt(variance + EPSILON)
    return centred * inv_std, inv_std


def pack_kernel(tok, cot, reg, to_up, to_left, to_diag, tok_v, cot_v, reg_v, sem):
    copies = [
        pltpu.make_async_copy(src, dst, sem.at[k])
        for k, (src, dst) in enumerate(((tok, tok_v), (cot, cot_v), (reg, reg_v)))
    ]
    for copy in copies:
        copy.start()
    to_up[96:112] = jnp.zeros((16, D), BF16)
    to_left[8] = jnp.zeros((4, D), BF16)
    to_diag[8] = jnp.zeros((4, D), BF16)
    for copy in copies:
        copy.wait()
    for k, src in ((0, tok_v), (4, cot_v)):
        for r in range(0, SHIFT, 2):
            first = src[r].astype(F32)
            second = src[r + 1].astype(F32)
            at = (k + r) * 12
            to_up[at : at + 24] = jnp.concatenate([first[4:16], second[4:16]], axis=0).astype(BF16)
        for r in range(SHIFT):
            to_diag[k + r] = src[r].astype(F32)[0:4].astype(BF16)
            to_left[k + r] = src[SHIFT + r].astype(F32)[0:4].astype(BF16)
    classes = reg_v[...].astype(F32)
    to_up[96:104, 0:16] = classes.astype(BF16)
    to_diag[8, 0:4, 0:16] = classes[0:4].astype(BF16)
    to_left[8, 0:4, 0:16] = classes[4:8].astype(BF16)


def bias_kernel(table_far, bucket_far, bias, bucket2, table, bucket, sem):
    copies = [
        pltpu.make_async_copy(table_far, table, sem.at[0]),
        pltpu.make_async_copy(bucket_far, bucket, sem.at[1]),
    ]
    for copy in copies:
        copy.start()
    for copy in copies:
        copy.wait()
    turned = jnp.concatenate([table[...], jnp.zeros((HEADS, 256 - NBIAS), F32)], axis=1)
    both = jnp.concatenate([bucket[...], bucket[...]], axis=1)
    bucket2[...] = jnp.where(iota((32, 128), 1) < 64, both[0:32], both[32:64])
    for block in range(AREA // 8):
        index = both[block * 8 : block * 8 + 8]
        upper = index >= 128
        within = jnp.bitwise_and(index, 127)
        for h in range(HEADS):
            first = jnp.broadcast_to(turned[h : h + 1, 0:128], (8, 128))
            second = jnp.broadcast_to(turned[h : h + 1, 128:256], (8, 128))
            got_first = jnp.take_along_axis(first, within, axis=1, mode="promise_in_bounds")
            got_second = jnp.take_along_axis(second, within, axis=1, mode="promise_in_bounds")
            bias[h, block * 8 : block * 8 + 8, :] = jnp.where(upper, got_second, got_first)


def window_kernel(
    tok_far, cot_far, reg_far, wqkv_far, wout_far, gain_far, bias, bucket2, up, left, diag,
    send, keep, own_grad, down_grad, right_grad, diag_grad,
    frame_t, frame_c, labels, packed, attended, grad_att, pairs, grad_in,
    tok, cot, reg, wqkv, wout, gain, sem,
):
    moves = (
        (tok_far, tok), (cot_far, cot), (reg_far, reg), (wqkv_far, wqkv),
        (wout_far, wout), (gain_far, gain),
    )
    copies = [pltpu.make_async_copy(src, dst, sem.at[k]) for k, (src, dst) in enumerate(moves)]
    for copy in copies:
        copy.start()
    for copy in copies[0:3]:
        copy.wait()

    up_f = up[...].astype(F32)
    for src, k, frame in ((tok, 0, frame_t), (cot, 4, frame_c)):
        for r in range(SHIFT):
            own = src[SHIFT + r].astype(F32)
            frame[r * 8 : r * 8 + 8, :] = own[4:12]
            frame[64 + r * 8 : 64 + r * 8 + 4, :] = own[12:16]
            frame[64 + r * 8 + 4 : 64 + r * 8 + 8, :] = left[k + r].astype(F32)
            s = SHIFT + r
            below = up_f[(k + r) * 12 : (k + r) * 12 + 12]
            frame[s * 8 : s * 8 + 8, :] = below[0:8]
            frame[64 + s * 8 : 64 + s * 8 + 4, :] = below[8:12]
            frame[64 + s * 8 + 4 : 64 + s * 8 + 8, :] = diag[k + r].astype(F32)

    mine = reg[...].astype(F32)
    labels[...] = jnp.zeros_like(labels)
    labels[0:4, 0:12] = mine[4:8, 4:16]
    labels[0:4, 12:16] = left[8, 0:4, 0:16].astype(F32)[:, 0:4]
    labels[4:8, 0:12] = up_f[96:100, 4:16]
    labels[4:8, 12:16] = diag[8, 0:4, 0:16].astype(F32)[:, 0:4]
    row_tile = (lax.axis_index("y") * 2 + lax.axis_index("zh")) * 2 + lax.axis_index("core")
    last = (row_tile == NROWS - 1).astype(F32)
    flags = jnp.where(iota((8, 128), 0) >= 4, 2.0, 0.0) * last
    coded = labels[...] + flags + jnp.where(iota((8, 128), 1) >= 8, 4.0, 0.0)
    token_lane = iota((128, 128), 1)
    token_row = iota((128, 128), 0)

    def column_of(token):
        return (token // 64) * 8 + token % 8

    def row_of(token):
        return (token // 8) % 8

    pick_lane = (column_of(token_lane) == token_row).astype(BF16)
    wide = dot(coded.astype(BF16), pick_lane)
    code_row = jnp.sum(
        jnp.where(row_of(iota((8, 128), 1)) == iota((8, 128), 0), wide, 0.0), axis=0, keepdims=True
    )
    pick_row = (column_of(token_row) == token_lane).astype(BF16)
    padded_codes = jnp.concatenate([coded, jnp.zeros((120, 128), F32)], axis=0).astype(BF16)
    tall = dot_nt(pick_row, padded_codes)
    code_col = jnp.sum(
        jnp.where(row_of(token_row) == token_lane, tall, 0.0), axis=1, keepdims=True
    )
    allowed = jnp.broadcast_to(code_col, (128, 128)) == jnp.broadcast_to(code_row, (128, 128))
    allowed4 = jnp.concatenate([allowed.astype(F32)] * GROUP, axis=0) > 0.5

    hat, _ = layer_stats(frame_t[...])
    copies[5].wait()
    normed = (hat * gain[...]).astype(BF16)
    cots = frame_c[...].astype(BF16)
    for copy in copies[3:5]:
        copy.wait()
    packed[...] = dot(normed, wqkv[...]).astype(BF16)
    grad_att[...] = dot_nt(cots, wout[...]).astype(BF16)
    send[0:TOKENS, 3 * D : 4 * D] = cots

    lane_head = iota((TOKENS, 128), 1) // HEAD_DIM
    masks = [lane_head == h for h in range(GROUP)]

    def stacked(value):
        return jnp.concatenate(
            [jnp.where(m, value, jnp.zeros_like(value)) for m in masks], axis=0
        )

    def beside(value):
        return jnp.concatenate([value[h * 128 : h * 128 + 128] for h in range(GROUP)], axis=1)

    for g in range(HEADS // GROUP):
        at = g * 128
        query = packed[:, at : at + 128]
        key = packed[:, D + at : D + at + 128]
        value = packed[:, 2 * D + at : 2 * D + at + 128]
        outer = grad_att[:, at : at + 128]
        query_s = stacked(query)
        outer_s = stacked(outer)
        biases = []
        for h in range(GROUP):
            one = bias[g * GROUP + h]
            biases += [one, one]
        scores = dot_nt(query_s, key) * SCALE + jnp.concatenate(biases, axis=0)
        scores = jnp.where(allowed4, scores, -1e30)
        raised = jnp.exp(scores - jnp.max(scores, axis=-1, keepdims=True))
        probs = raised / jnp.sum(raised, axis=-1, keepdims=True)
        probs_low = probs.astype(BF16)
        grad_probs = dot_nt(outer_s, value)
        inner = probs * grad_probs
        grad_scores = probs * (grad_probs - jnp.sum(inner, axis=-1, keepdims=True))
        grad_scaled = (grad_scores * SCALE).astype(BF16)
        attended[:, at : at + 128] = dot(beside(probs_low), stacked(value)).astype(BF16)
        send[0:TOKENS, at : at + 128] = dot(beside(grad_scaled), stacked(key)).astype(BF16)
        send[0:TOKENS, D + at : D + at + 128] = dot_tn(grad_scaled, query_s).astype(BF16)
        send[0:TOKENS, 2 * D + at : 2 * D + at + 128] = dot_tn(probs_low, outer_s).astype(BF16)
        for h in range(GROUP):
            one = grad_scores[h * 128 : h * 128 + 128]
            pairs[g * GROUP + h] = (one[0:32] + one[96:128]) + pltpu.roll(
                one[32:64] + one[64:96], 64, 1
            )

    core = lax.axis_index("core")
    for k, matrix in ((0, normed), (1, attended[...])):
        turned = matrix.astype(F32).T.reshape(16, 2, 16, TOKENS)
        even, odd = turned[:, 0].reshape(256, TOKENS), turned[:, 1].reshape(256, TOKENS)
        kept = jnp.where(core == 0, even, odd).astype(BF16)
        sent = jnp.where(core == 0, odd, even).astype(BF16)
        for b in range(2):
            lane = (2 * k + b) * 128
            keep[:, lane : lane + 128] = kept[b * 128 : b * 128 + 128]
            send[0:TOKENS, 4 * D + lane : 4 * D + lane + 128] = sent[b * 128 : b * 128 + 128]

    grad_normed = dot_nt(send[0:TOKENS, 0 : 3 * D], wqkv[...])
    grad_in[...] = grad_normed
    gain_sum = jnp.sum(grad_normed * hat, axis=0, keepdims=True)

    bucket_of = iota((256, 128), 0)
    step = 2

    def add_rows(k, total):
        parts, hots = [], []
        for t in range(step):
            i = k * step + t
            parts.append(pairs[:, i, :])
            which = jnp.broadcast_to(bucket2[pl.ds(i, 1), :], (256, 128))
            hots.append((bucket_of == which).astype(BF16))
        high, low = split_high_low(jnp.concatenate(parts, axis=1))
        both = jnp.concatenate([high, low], axis=0)
        return total + dot_nt(both, jnp.concatenate(hots, axis=1))

    sums = lax.fori_loop(
        0, AREA // 2 // step, add_rows, jnp.zeros((2 * HEADS, 256), F32), unroll=True
    )
    table = sums[0:HEADS] + sums[HEADS : 2 * HEADS]
    high, low = split_high_low(table)
    send[TOKENS : TOKENS + 16, 0:256] = high
    send[TOKENS : TOKENS + 16, 256:512] = low
    high, low = split_high_low(jnp.concatenate([gain_sum, jnp.zeros((15, D), F32)], axis=0))
    send[TOKENS : TOKENS + 16, 512:1024] = high
    send[TOKENS : TOKENS + 16, 1024:1536] = low
    send[TOKENS : TOKENS + 16, 1536:2560] = jnp.zeros((16, 1024), BF16)

    for r in range(SHIFT):
        s = SHIFT + r
        own_grad[r, 0:8, :] = grad_in[r * 8 : r * 8 + 8, :]
        own_grad[r, 8:12, :] = grad_in[64 + r * 8 : 64 + r * 8 + 4, :]
        right_grad[r] = grad_in[64 + r * 8 : 64 + r * 8 + 8, :][4:8].astype(BF16)
        down_grad[r] = jnp.concatenate(
            [grad_in[s * 8 : s * 8 + 8, :], grad_in[64 + s * 8 : 64 + s * 8 + 8, :][0:4]], axis=0
        ).astype(BF16)
        diag_grad[r] = grad_in[64 + s * 8 : 64 + s * 8 + 8, :][4:8].astype(BF16)


def product_kernel(mine, other, keep, out):
    def rows(block):
        lane = block * 128
        return jnp.concatenate(
            [keep[:, lane : lane + 128], other[0:TOKENS, 4 * D + lane : 4 * D + lane + 128]], axis=1
        )

    right = jnp.concatenate([mine[0:TOKENS, 0 : 4 * D], other[0:TOKENS, 0 : 4 * D]], axis=0)
    for half in range(2):
        at = half * 128
        qkv = dot(rows(half), right[:, 0 : 3 * D]).astype(BF16)
        proj = dot(rows(2 + half), right[:, 3 * D : 4 * D]).astype(BF16)
        for x in range(4):
            out[x, at : at + 128, 0:384] = qkv[:, x * 384 : x * 384 + 384]
            out[x, at : at + 128, 384:512] = proj[:, x * 128 : x * 128 + 128]
    small = mine[TOKENS : TOKENS + 16, 0:1536].astype(F32) + other[TOKENS : TOKENS + 16, 0:1536].astype(F32)
    table = small[:, 0:256] + small[:, 256:512]
    gain = small[0:8, 512:1024] + small[0:8, 1024:1536]
    for x in range(4):
        part = jnp.concatenate(
            [
                table[4 * x : 4 * x + 4, 0:128],
                table[4 * x : 4 * x + 4, 128:256],
                gain[:, x * 128 : x * 128 + 128],
            ],
            axis=0,
        )
        high, low = split_high_low(part)
        out[x, 256:272, 0:128] = high
        out[x, 256:272, 128:256] = low
        out[x, 256:272, 256:512] = jnp.zeros((16, 256), BF16)


def across_sum_kernel(parts, out):
    small = jnp.sum(parts[:, 256:272, 0:256].astype(F32), axis=0)
    high, low = split_high_low(small[:, 0:128] + small[:, 128:256])
    both = jnp.concatenate([high, low], axis=0)
    for y in range(8):
        total = jnp.sum(parts[:, y * 32 : y * 32 + 32, :].astype(F32), axis=0)
        out[y, :, 0:512] = total.astype(BF16)
        out[y, :, 512:640] = both


def plane_sum_kernel(parts, out):
    total = jnp.sum(parts[...].astype(F32), axis=0)
    small = (total[0:16, 512:640] + total[16:32, 512:640]).astype(BF16)
    for zh in range(2):
        rows = total[zh * 16 : zh * 16 + 16]
        proj = rows[:, 384:512].astype(BF16)
        for zl in range(6):
            lane = (zl // 2) * 128
            qkv = rows[:, lane : lane + 128]
            if zl % 2 == 1:
                qkv = pltpu.roll(qkv, 64, 1)
            out[zh * 6 + zl, :, 0:128] = proj
            out[zh * 6 + zl, :, 128:256] = qkv.astype(BF16)
            out[zh * 6 + zl, :, 256:384] = small


def line_sum_kernel(parts, qkv, out):
    total = jnp.sum(parts[...].astype(F32), axis=0)
    qkv[...] = total[:, 128:192]
    for x in range(4):
        out[x, 0:16, :] = total[:, 0:128]
        out[x, 16:32, :] = total[:, 256:384]


def finish_kernel(parts, proj, gain, table):
    low, high = [], []
    for x in range(4):
        proj[:, x * 128 : x * 128 + 128] = parts[x, 0:16, :]
        gain[:, x * 128 : x * 128 + 128] = parts[x, 24:25, :]
        low.append(parts[x, 16:20, :])
        high.append(parts[x, 20:24, :])
    table[:, 0:128] = jnp.concatenate(low, axis=0)
    table[:, 128:NBIAS] = jnp.concatenate(high, axis=0)[:, 0 : NBIAS - 128]


def token_kernel(tok, cot, gain, own, above, left, diag, out, grads):
    for r in range(SHIFT):
        grads[r, 0:4, :] = diag[r].astype(F32)
        grads[r, 4:16, :] = above[r].astype(F32)
        grads[SHIFT + r, 0:4, :] = left[r].astype(F32)
        grads[SHIFT + r, 4:16, :] = own[r]
    hat, inv_std = layer_stats(tok[...].astype(F32))
    grad_hat = grads[...] * gain[...].reshape(1, 1, D)
    moved = (
        grad_hat
        - jnp.mean(grad_hat, axis=-1, keepdims=True)
        - hat * jnp.mean(grad_hat * hat, axis=-1, keepdims=True)
    )
    out[...] = (cot[...].astype(F32) + inv_std * moved).astype(BF16)


def shape(dims, dtype):
    return jax.ShapeDtypeStruct(dims, dtype)


def call(kernel, outs, args, scratch=(), flops=0, moved=0, remain=(), params=ANY_PARAMS):
    args = [
        pltpu.with_memory_space_constraint(arg, pltpu.HBM) if k in remain else arg
        for k, arg in enumerate(args)
    ]
    return pl.pallas_call(
        kernel,
        in_specs=[
            pl.BlockSpec(memory_space=pltpu.HBM if k in remain else pltpu.VMEM)
            for k in range(len(args))
        ],
        out_shape=outs,
        scratch_shapes=list(scratch),
        compiler_params=params,
        cost_estimate=pl.CostEstimate(flops=flops, bytes_accessed=moved, transcendentals=0),
    )(*args)


def neighbour(value, down, right):
    pairs = [
        (r * NCOLS + c, ((r + down) % NROWS) * NCOLS + (c + right) % NCOLS)
        for r in range(NROWS)
        for c in range(NCOLS)
    ]
    return lax.ppermute(value, ROWS + COLS, pairs)


def local(tokens, cotangent, region, norm_gain, qkv_weight, out_weight, bias_table, bias_bucket):
    gain = norm_gain.reshape(1, D)
    to_up, to_left, to_diag = call(
        pack_kernel,
        [shape((112, D), BF16), shape((9, 4, D), BF16), shape((9, 4, D), BF16)],
        (tokens, cotangent, region),
        [
            pltpu.VMEM((8, 16, D), BF16),
            pltpu.VMEM((8, 16, D), BF16),
            pltpu.VMEM((8, 16), jnp.int32),
            pltpu.SemaphoreType.DMA((3,)),
        ],
        moved=1 << 19,
        remain=(0, 1, 2),
    )
    up = neighbour(to_up, -1, 0)
    diag = neighbour(to_diag, -1, -1)
    left = neighbour(to_left, 0, -1)
    bias, bucket2 = call(
        bias_kernel,
        [
            shape((HEADS, AREA, 128), F32),
            shape((AREA // 2, 128), jnp.int32),
        ],
        (bias_table.T, bias_bucket),
        [
            pltpu.VMEM((HEADS, NBIAS), F32),
            pltpu.VMEM((AREA, AREA), jnp.int32),
            pltpu.SemaphoreType.DMA((2,)),
        ],
        moved=1 << 23,
        remain=(0, 1),
    )
    send, keep, own_grad, down_grad, right_grad, diag_grad = call(
        window_kernel,
        [
            shape((TOKENS + 16, 5 * D), BF16),
            shape((TOKENS, D), BF16),
            shape((4, 12, D), F32),
            shape((4, 12, D), BF16),
            shape((4, 4, D), BF16),
            shape((4, 4, D), BF16),
        ],
        (tokens, cotangent, region, qkv_weight, out_weight, gain, bias, bucket2, up, left, diag),
        [
            pltpu.VMEM((TOKENS, D), F32),
            pltpu.VMEM((TOKENS, D), F32),
            pltpu.VMEM((8, 128), F32),
            pltpu.VMEM((TOKENS, 3 * D), BF16),
            pltpu.VMEM((TOKENS, D), BF16),
            pltpu.VMEM((TOKENS, D), BF16),
            pltpu.VMEM((HEADS, AREA // 2, 128), F32),
            pltpu.VMEM((TOKENS, D), F32),
            pltpu.VMEM((8, 16, D), BF16),
            pltpu.VMEM((8, 16, D), BF16),
            pltpu.VMEM((8, 16), jnp.int32),
            pltpu.VMEM((D, 3 * D), BF16),
            pltpu.VMEM((D, D), BF16),
            pltpu.VMEM((1, D), F32),
            pltpu.SemaphoreType.DMA((6,)),
        ],
        flops=1 << 30,
        moved=1 << 23,
        remain=tuple(range(6)),
    )
    other = lax.ppermute(send, "core", [(0, 1), (1, 0)])
    products = call(
        product_kernel,
        shape((4, 272, D), BF16),
        (send, other, keep),
        flops=1 << 29,
        moved=1 << 21,
    )
    products, down_grad = lax.optimization_barrier((products, down_grad))
    across = lax.all_to_all(products, "x", 0, 0)
    above_grad = neighbour(down_grad, 1, 0)
    halves = call(across_sum_kernel, shape((8, 32, 640), BF16), (across,), moved=1 << 21)
    halves, above_grad, right_grad, diag_grad = lax.optimization_barrier(
        (halves, above_grad, right_grad, diag_grad)
    )
    planes = lax.all_to_all(halves, "y", 0, 0)
    left_grad = neighbour(right_grad, 0, 1)
    corner_grad = neighbour(diag_grad, 1, 1)
    chunks = call(plane_sum_kernel, shape((12, 16, 384), BF16), (planes,), moved=1 << 21)
    chunks, left_grad, corner_grad = lax.optimization_barrier((chunks, left_grad, corner_grad))
    lines = lax.all_to_all(chunks, ("zh", "zl"), 0, 0)
    grad_qkv, finals = call(
        line_sum_kernel, [shape((16, 64), F32), shape((4, 32, 128), F32)], (lines,), moved=1 << 18
    )
    finals = lax.all_to_all(finals, "x", 0, 0)
    grad_tokens = call(
        token_kernel,
        shape((8, 16, D), BF16),
        (tokens, cotangent, gain, own_grad, above_grad, left_grad, corner_grad),
        [pltpu.VMEM((8, 16, D), F32)],
        moved=1 << 20,
    )
    grad_out_weight, grad_gain, grad_bias_table = call(
        finish_kernel,
        [shape((16, D), F32), shape((1, D), F32), shape((HEADS, NBIAS), F32)],
        (finals,),
        moved=1 << 17,
    )
    return (grad_tokens, grad_qkv, grad_out_weight, grad_gain.reshape(D), grad_bias_table.T)


def solution(mesh):
    parts = Mesh(mesh.devices.reshape([n for _, n in PARTS]), [name for name, _ in PARTS])
    return jax.shard_map(
        local,
        mesh=parts,
        in_specs=(P(ROWS, COLS, None), P(ROWS, COLS, None), P(ROWS, COLS), P(), P(), P(), P(), P()),
        out_specs=(P(ROWS, COLS, None), P(ROWS, COLS), P(ROWS, None), P(), P()),
        check_vma=False,
    )
```

```python
import jax
import jax.numpy as jnp
from jax import lax
from jax.experimental import pallas as pl
from jax.experimental.pallas import tpu as pltpu
from jax.sharding import Mesh
from jax.sharding import PartitionSpec as P

D = 512
HEADS = 16
HEAD_DIM = 32
WIN = 8
SHIFT = 4
NBIAS = 225
AREA = WIN * WIN
TOKENS = 128
GROUP = 4
SCALE = HEAD_DIM ** (-0.5)
EPSILON = 1e-05

F32 = jnp.float32
BF16 = jnp.bfloat16

PARTS = (("y", 8), ("zh", 2), ("core", 2), ("x", 4), ("zl", 6))
ROWS = ("y", "zh", "core")
COLS = ("x", "zl")
NROWS = 32
NCOLS = 24

ANY_PARAMS = pltpu.CompilerParams(vmem_limit_bytes=48 * 1024 * 1024)


def dot(a, b):
    return lax.dot_general(a, b, (((1,), (0,)), ((), ())), preferred_element_type=F32)


def dot_nt(a, b):
    return lax.dot_general(a, b, (((1,), (1,)), ((), ())), preferred_element_type=F32)


def dot_tn(a, b):
    return lax.dot_general(a, b, (((0,), (0,)), ((), ())), preferred_element_type=F32)


def iota(shape, dim):
    return lax.broadcasted_iota(jnp.int32, shape, dim)


def split_high_low(value):
    high = value.astype(BF16)
    low = (value - high.astype(F32)).astype(BF16)
    return high, low


def layer_stats(floats):
    average = jnp.mean(floats, axis=-1, keepdims=True)
    centred = floats - average
    variance = jnp.mean(centred * centred, axis=-1, keepdims=True)
    inv_std = lax.rsqrt(variance + EPSILON)
    return centred * inv_std, inv_std


def pack_kernel(tok, cot, reg, to_up, to_left, to_diag, tok_v, cot_v, reg_v, sem):
    copies = [
        pltpu.make_async_copy(src, dst, sem.at[k])
        for k, (src, dst) in enumerate(((tok, tok_v), (cot, cot_v), (reg, reg_v)))
    ]
    for copy in copies:
        copy.start()
    to_up[96:112] = jnp.zeros((16, D), BF16)
    to_left[8] = jnp.zeros((4, D), BF16)
    to_diag[8] = jnp.zeros((4, D), BF16)
    for copy in copies:
        copy.wait()
    for k, src in ((0, tok_v), (4, cot_v)):
        for r in range(0, SHIFT, 2):
            first = src[r].astype(F32)
            second = src[r + 1].astype(F32)
            at = (k + r) * 12
            to_up[at : at + 24] = jnp.concatenate([first[4:16], second[4:16]], axis=0).astype(BF16)
        for r in range(SHIFT):
            to_diag[k + r] = src[r].astype(F32)[0:4].astype(BF16)
            to_left[k + r] = src[SHIFT + r].astype(F32)[0:4].astype(BF16)
    classes = reg_v[...].astype(F32)
    to_up[96:104, 0:16] = classes.astype(BF16)
    to_diag[8, 0:4, 0:16] = classes[0:4].astype(BF16)
    to_left[8, 0:4, 0:16] = classes[4:8].astype(BF16)


def bias_kernel(table_far, bucket_far, bias, bucket2, table, bucket, sem):
    copies = [
        pltpu.make_async_copy(table_far, table, sem.at[0]),
        pltpu.make_async_copy(bucket_far, bucket, sem.at[1]),
    ]
    for copy in copies:
        copy.start()
    for copy in copies:
        copy.wait()
    turned = jnp.concatenate([table[...], jnp.zeros((HEADS, 256 - NBIAS), F32)], axis=1)
    both = jnp.concatenate([bucket[...], bucket[...]], axis=1)
    bucket2[...] = jnp.where(iota((32, 128), 1) < 64, both[0:32], both[32:64])
    for block in range(AREA // 8):
        index = both[block * 8 : block * 8 + 8]
        upper = index >= 128
        within = jnp.bitwise_and(index, 127)
        for h in range(HEADS):
            first = jnp.broadcast_to(turned[h : h + 1, 0:128], (8, 128))
            second = jnp.broadcast_to(turned[h : h + 1, 128:256], (8, 128))
            got_first = jnp.take_along_axis(first, within, axis=1, mode="promise_in_bounds")
            got_second = jnp.take_along_axis(second, within, axis=1, mode="promise_in_bounds")
            bias[h, block * 8 : block * 8 + 8, :] = jnp.where(upper, got_second, got_first)


def window_kernel(
    tok_far, cot_far, reg_far, wqkv_far, wout_far, gain_far, bias, bucket2, up, left, diag,
    send, keep, own_grad, down_grad, right_grad, diag_grad,
    frame_t, frame_c, labels, packed, attended, grad_att, pairs, grad_in,
    tok, cot, reg, wqkv, wout, gain, sem,
):
    moves = (
        (tok_far, tok), (cot_far, cot), (reg_far, reg), (wqkv_far, wqkv),
        (wout_far, wout), (gain_far, gain),
    )
    copies = [pltpu.make_async_copy(src, dst, sem.at[k]) for k, (src, dst) in enumerate(moves)]
    for copy in copies:
        copy.start()
    for copy in copies[0:3]:
        copy.wait()

    up_f = up[...].astype(F32)
    for src, k, frame in ((tok, 0, frame_t), (cot, 4, frame_c)):
        for r in range(SHIFT):
            own = src[SHIFT + r].astype(F32)
            frame[r * 8 : r * 8 + 8, :] = own[4:12]
            frame[64 + r * 8 : 64 + r * 8 + 4, :] = own[12:16]
            frame[64 + r * 8 + 4 : 64 + r * 8 + 8, :] = left[k + r].astype(F32)
            s = SHIFT + r
            below = up_f[(k + r) * 12 : (k + r) * 12 + 12]
            frame[s * 8 : s * 8 + 8, :] = below[0:8]
            frame[64 + s * 8 : 64 + s * 8 + 4, :] = below[8:12]
            frame[64 + s * 8 + 4 : 64 + s * 8 + 8, :] = diag[k + r].astype(F32)

    mine = reg[...].astype(F32)
    labels[...] = jnp.zeros_like(labels)
    labels[0:4, 0:12] = mine[4:8, 4:16]
    labels[0:4, 12:16] = left[8, 0:4, 0:16].astype(F32)[:, 0:4]
    labels[4:8, 0:12] = up_f[96:100, 4:16]
    labels[4:8, 12:16] = diag[8, 0:4, 0:16].astype(F32)[:, 0:4]
    row_tile = (lax.axis_index("y") * 2 + lax.axis_index("zh")) * 2 + lax.axis_index("core")
    last = (row_tile == NROWS - 1).astype(F32)
    flags = jnp.where(iota((8, 128), 0) >= 4, 2.0, 0.0) * last
    coded = labels[...] + flags + jnp.where(iota((8, 128), 1) >= 8, 4.0, 0.0)
    token_lane = iota((128, 128), 1)
    token_row = iota((128, 128), 0)

    def column_of(token):
        return (token // 64) * 8 + token % 8

    def row_of(token):
        return (token // 8) % 8

    pick_lane = (column_of(token_lane) == token_row).astype(BF16)
    wide = dot(coded.astype(BF16), pick_lane)
    code_row = jnp.sum(
        jnp.where(row_of(iota((8, 128), 1)) == iota((8, 128), 0), wide, 0.0), axis=0, keepdims=True
    )
    pick_row = (column_of(token_row) == token_lane).astype(BF16)
    padded_codes = jnp.concatenate([coded, jnp.zeros((120, 128), F32)], axis=0).astype(BF16)
    tall = dot_nt(pick_row, padded_codes)
    code_col = jnp.sum(
        jnp.where(row_of(token_row) == token_lane, tall, 0.0), axis=1, keepdims=True
    )
    allowed = jnp.broadcast_to(code_col, (128, 128)) == jnp.broadcast_to(code_row, (128, 128))
    allowed4 = jnp.concatenate([allowed.astype(F32)] * GROUP, axis=0) > 0.5

    hat, _ = layer_stats(frame_t[...])
    copies[5].wait()
    normed = (hat * gain[...]).astype(BF16)
    cots = frame_c[...].astype(BF16)
    for copy in copies[3:5]:
        copy.wait()
    packed[...] = dot(normed, wqkv[...]).astype(BF16)
    grad_att[...] = dot_nt(cots, wout[...]).astype(BF16)
    send[0:TOKENS, 3 * D : 4 * D] = cots

    lane_head = iota((TOKENS, 128), 1) // HEAD_DIM
    masks = [lane_head == h for h in range(GROUP)]

    def stacked(value):
        return jnp.concatenate(
            [jnp.where(m, value, jnp.zeros_like(value)) for m in masks], axis=0
        )

    def beside(value):
        return jnp.concatenate([value[h * 128 : h * 128 + 128] for h in range(GROUP)], axis=1)

    for g in range(HEADS // GROUP):
        at = g * 128
        query = packed[:, at : at + 128]
        key = packed[:, D + at : D + at + 128]
        value = packed[:, 2 * D + at : 2 * D + at + 128]
        outer = grad_att[:, at : at + 128]
        query_s = stacked(query)
        outer_s = stacked(outer)
        biases = []
        for h in range(GROUP):
            one = bias[g * GROUP + h]
            biases += [one, one]
        scores = dot_nt(query_s, key) * SCALE + jnp.concatenate(biases, axis=0)
        scores = jnp.where(allowed4, scores, -1e30)
        raised = jnp.exp(scores - jnp.max(scores, axis=-1, keepdims=True))
        probs = raised / jnp.sum(raised, axis=-1, keepdims=True)
        probs_low = probs.astype(BF16)
        grad_probs = dot_nt(outer_s, value)
        inner = probs * grad_probs
        grad_scores = probs * (grad_probs - jnp.sum(inner, axis=-1, keepdims=True))
        grad_scaled = (grad_scores * SCALE).astype(BF16)
        attended[:, at : at + 128] = dot(beside(probs_low), stacked(value)).astype(BF16)
        send[0:TOKENS, at : at + 128] = dot(beside(grad_scaled), stacked(key)).astype(BF16)
        send[0:TOKENS, D + at : D + at + 128] = dot_tn(grad_scaled, query_s).astype(BF16)
        send[0:TOKENS, 2 * D + at : 2 * D + at + 128] = dot_tn(probs_low, outer_s).astype(BF16)
        for h in range(GROUP):
            one = grad_scores[h * 128 : h * 128 + 128]
            pairs[g * GROUP + h] = (one[0:32] + one[96:128]) + pltpu.roll(
                one[32:64] + one[64:96], 64, 1
            )

    core = lax.axis_index("core")
    for k, matrix in ((0, normed), (1, attended[...])):
        turned = matrix.astype(F32).T.reshape(16, 2, 16, TOKENS)
        even, odd = turned[:, 0].reshape(256, TOKENS), turned[:, 1].reshape(256, TOKENS)
        kept = jnp.where(core == 0, even, odd).astype(BF16)
        sent = jnp.where(core == 0, odd, even).astype(BF16)
        for b in range(2):
            lane = (2 * k + b) * 128
            keep[:, lane : lane + 128] = kept[b * 128 : b * 128 + 128]
            send[0:TOKENS, 4 * D + lane : 4 * D + lane + 128] = sent[b * 128 : b * 128 + 128]

    grad_normed = dot_nt(send[0:TOKENS, 0 : 3 * D], wqkv[...])
    grad_in[...] = grad_normed
    gain_sum = jnp.sum(grad_normed * hat, axis=0, keepdims=True)

    bucket_of = iota((256, 128), 0)
    step = 2

    def add_rows(k, total):
        parts, hots = [], []
        for t in range(step):
            i = k * step + t
            parts.append(pairs[:, i, :])
            which = jnp.broadcast_to(bucket2[pl.ds(i, 1), :], (256, 128))
            hots.append((bucket_of == which).astype(BF16))
        high, low = split_high_low(jnp.concatenate(parts, axis=1))
        both = jnp.concatenate([high, low], axis=0)
        return total + dot_nt(both, jnp.concatenate(hots, axis=1))

    sums = lax.fori_loop(
        0, AREA // 2 // step, add_rows, jnp.zeros((2 * HEADS, 256), F32), unroll=True
    )
    table = sums[0:HEADS] + sums[HEADS : 2 * HEADS]
    high, low = split_high_low(table)
    send[TOKENS : TOKENS + 16, 0:256] = high
    send[TOKENS : TOKENS + 16, 256:512] = low
    high, low = split_high_low(jnp.concatenate([gain_sum, jnp.zeros((15, D), F32)], axis=0))
    send[TOKENS : TOKENS + 16, 512:1024] = high
    send[TOKENS : TOKENS + 16, 1024:1536] = low
    send[TOKENS : TOKENS + 16, 1536:2560] = jnp.zeros((16, 1024), BF16)

    for r in range(SHIFT):
        s = SHIFT + r
        own_grad[r, 0:8, :] = grad_in[r * 8 : r * 8 + 8, :]
        own_grad[r, 8:12, :] = grad_in[64 + r * 8 : 64 + r * 8 + 4, :]
        right_grad[r] = grad_in[64 + r * 8 : 64 + r * 8 + 8, :][4:8].astype(BF16)
        down_grad[r] = jnp.concatenate(
            [grad_in[s * 8 : s * 8 + 8, :], grad_in[64 + s * 8 : 64 + s * 8 + 8, :][0:4]], axis=0
        ).astype(BF16)
        diag_grad[r] = grad_in[64 + s * 8 : 64 + s * 8 + 8, :][4:8].astype(BF16)


def product_kernel(mine, other, keep, out):
    def rows(block):
        lane = block * 128
        return jnp.concatenate(
            [keep[:, lane : lane + 128], other[0:TOKENS, 4 * D + lane : 4 * D + lane + 128]], axis=1
        )

    right = jnp.concatenate([mine[0:TOKENS, 0 : 4 * D], other[0:TOKENS, 0 : 4 * D]], axis=0)
    for half in range(2):
        qkv = dot(rows(half), right[:, 0 : 3 * D]).astype(BF16)
        proj = dot(rows(2 + half), right[:, 3 * D : 4 * D]).astype(BF16)
        for k in range(4):
            for x in range(4):
                to = (half * 4 + k) * 4 + x
                at = k * 32
                for block in range(3):
                    lane = x * 384 + block * 128
                    out[to, block * 32 : block * 32 + 32, :] = qkv[at : at + 32, lane : lane + 128]
                out[to, 96:128, :] = proj[at : at + 32, x * 128 : x * 128 + 128]
    first = lax.axis_index("core") == 0
    small = mine[TOKENS : TOKENS + 16, 0:1536].astype(F32) + other[TOKENS : TOKENS + 16, 0:1536].astype(F32)
    table = small[:, 0:256] + small[:, 256:512]
    table = jnp.where(first, table[0:8], table[8:16])
    gain = small[0:8, 512:1024] + small[0:8, 1024:1536]
    gain = jnp.where(first, gain[:, 0:256], gain[:, 256:512])
    for x in range(4):
        lane = (x // 2) * 128
        piece = gain[:, lane : lane + 128]
        if x % 2 == 1:
            piece = pltpu.roll(piece, 64, 1)
        part = jnp.concatenate(
            [table[2 * x : 2 * x + 2, 0:128], table[2 * x : 2 * x + 2, 128:256], piece[0:4]], axis=0
        ).astype(BF16)
        for y in range(8):
            out[y * 4 + x, 128:136, :] = part


def plane_sum_kernel(parts, out):
    total = jnp.sum(parts[...].astype(F32), axis=0)
    left_half = iota((8, 128), 1) < 64
    small = total[128:136]
    for zh in range(2):
        proj = total[96 + zh * 16 : 112 + zh * 16].astype(BF16)
        for zl in range(6):
            at = (zl // 2) * 32 + zh * 16
            upper, lower = total[at : at + 8], total[at + 8 : at + 16]
            if zl % 2 == 0:
                lower = pltpu.roll(lower, 64, 1)
            else:
                upper = pltpu.roll(upper, 64, 1)
            qkv = jnp.where(left_half, upper, lower)
            out[zh * 6 + zl, 0:16, :] = proj
            out[zh * 6 + zl, 16:32, :] = jnp.concatenate([qkv, small], axis=0).astype(BF16)


def line_sum_kernel(parts, qkv, out):
    total = jnp.sum(parts[...].astype(F32), axis=0)
    qkv[0:8, :] = total[16:24, 0:64]
    qkv[8:16, :] = pltpu.roll(total[16:24], 64, 1)[:, 0:64]
    for to in range(8):
        out[to, 0:16, :] = total[0:16]
        out[to, 16:24, :] = total[24:32]


def finish_kernel(parts, proj, gain, table):
    core = lax.axis_index("core")
    for x in range(4):
        proj[:, x * 128 : x * 128 + 128] = parts[core * 4 + x, 0:16, :]
    left_half = iota((1, 128), 1) < 64
    low, high = [], []
    for k in range(8):
        low.append(parts[k, 16:18, :])
        high.append(parts[k, 18:20, :])
    for k in range(4):
        second = pltpu.roll(parts[2 * k + 1, 16:24, :], 64, 1)[4:5]
        gain[:, k * 128 : k * 128 + 128] = jnp.where(left_half, parts[2 * k, 20:21, :], second)
    table[:, 0:128] = jnp.concatenate(low, axis=0)
    table[:, 128:NBIAS] = jnp.concatenate(high, axis=0)[:, 0 : NBIAS - 128]


def token_kernel(tok, cot, gain, own, above, left, diag, out, grads):
    for r in range(SHIFT):
        grads[r, 0:4, :] = diag[r].astype(F32)
        grads[r, 4:16, :] = above[r].astype(F32)
        grads[SHIFT + r, 0:4, :] = left[r].astype(F32)
        grads[SHIFT + r, 4:16, :] = own[r]
    hat, inv_std = layer_stats(tok[...].astype(F32))
    grad_hat = grads[...] * gain[...].reshape(1, 1, D)
    moved = (
        grad_hat
        - jnp.mean(grad_hat, axis=-1, keepdims=True)
        - hat * jnp.mean(grad_hat * hat, axis=-1, keepdims=True)
    )
    out[...] = (cot[...].astype(F32) + inv_std * moved).astype(BF16)


def shape(dims, dtype):
    return jax.ShapeDtypeStruct(dims, dtype)


def call(kernel, outs, args, scratch=(), flops=0, moved=0, remain=(), params=ANY_PARAMS):
    args = [
        pltpu.with_memory_space_constraint(arg, pltpu.HBM) if k in remain else arg
        for k, arg in enumerate(args)
    ]
    return pl.pallas_call(
        kernel,
        in_specs=[
            pl.BlockSpec(memory_space=pltpu.HBM if k in remain else pltpu.VMEM)
            for k in range(len(args))
        ],
        out_shape=outs,
        scratch_shapes=list(scratch),
        compiler_params=params,
        cost_estimate=pl.CostEstimate(flops=flops, bytes_accessed=moved, transcendentals=0),
    )(*args)


def neighbour(value, down, right):
    pairs = [
        (r * NCOLS + c, ((r + down) % NROWS) * NCOLS + (c + right) % NCOLS)
        for r in range(NROWS)
        for c in range(NCOLS)
    ]
    return lax.ppermute(value, ROWS + COLS, pairs)


def local(tokens, cotangent, region, norm_gain, qkv_weight, out_weight, bias_table, bias_bucket):
    gain = norm_gain.reshape(1, D)
    to_up, to_left, to_diag = call(
        pack_kernel,
        [shape((112, D), BF16), shape((9, 4, D), BF16), shape((9, 4, D), BF16)],
        (tokens, cotangent, region),
        [
            pltpu.VMEM((8, 16, D), BF16),
            pltpu.VMEM((8, 16, D), BF16),
            pltpu.VMEM((8, 16), jnp.int32),
            pltpu.SemaphoreType.DMA((3,)),
        ],
        moved=1 << 19,
        remain=(0, 1, 2),
    )
    up = neighbour(to_up, -1, 0)
    diag = neighbour(to_diag, -1, -1)
    left = neighbour(to_left, 0, -1)
    bias, bucket2 = call(
        bias_kernel,
        [
            shape((HEADS, AREA, 128), F32),
            shape((AREA // 2, 128), jnp.int32),
        ],
        (bias_table.T, bias_bucket),
        [
            pltpu.VMEM((HEADS, NBIAS), F32),
            pltpu.VMEM((AREA, AREA), jnp.int32),
            pltpu.SemaphoreType.DMA((2,)),
        ],
        moved=1 << 23,
        remain=(0, 1),
    )
    send, keep, own_grad, down_grad, right_grad, diag_grad = call(
        window_kernel,
        [
            shape((TOKENS + 16, 5 * D), BF16),
            shape((TOKENS, D), BF16),
            shape((4, 12, D), F32),
            shape((4, 12, D), BF16),
            shape((4, 4, D), BF16),
            shape((4, 4, D), BF16),
        ],
        (tokens, cotangent, region, qkv_weight, out_weight, gain, bias, bucket2, up, left, diag),
        [
            pltpu.VMEM((TOKENS, D), F32),
            pltpu.VMEM((TOKENS, D), F32),
            pltpu.VMEM((8, 128), F32),
            pltpu.VMEM((TOKENS, 3 * D), BF16),
            pltpu.VMEM((TOKENS, D), BF16),
            pltpu.VMEM((TOKENS, D), BF16),
            pltpu.VMEM((HEADS, AREA // 2, 128), F32),
            pltpu.VMEM((TOKENS, D), F32),
            pltpu.VMEM((8, 16, D), BF16),
            pltpu.VMEM((8, 16, D), BF16),
            pltpu.VMEM((8, 16), jnp.int32),
            pltpu.VMEM((D, 3 * D), BF16),
            pltpu.VMEM((D, D), BF16),
            pltpu.VMEM((1, D), F32),
            pltpu.SemaphoreType.DMA((6,)),
        ],
        flops=1 << 30,
        moved=1 << 23,
        remain=tuple(range(6)),
    )
    other = lax.ppermute(send, "core", [(0, 1), (1, 0)])
    products = call(
        product_kernel,
        shape((32, 136, 128), BF16),
        (send, other, keep),
        flops=1 << 29,
        moved=1 << 21,
    )
    products, down_grad, right_grad, diag_grad = lax.optimization_barrier(
        (products, down_grad, right_grad, diag_grad)
    )
    planes = lax.all_to_all(products, ("y", "x"), 0, 0)
    above_grad = neighbour(down_grad, 1, 0)
    left_grad = neighbour(right_grad, 0, 1)
    corner_grad = neighbour(diag_grad, 1, 1)
    chunks = call(plane_sum_kernel, shape((12, 32, 128), BF16), (planes,), moved=1 << 21)
    chunks, above_grad, left_grad, corner_grad = lax.optimization_barrier(
        (chunks, above_grad, left_grad, corner_grad)
    )
    lines = lax.all_to_all(chunks, ("zh", "zl"), 0, 0)
    grad_qkv, finals = call(
        line_sum_kernel, [shape((16, 64), F32), shape((8, 24, 128), F32)], (lines,), moved=1 << 18
    )
    finals = lax.all_to_all(finals, ("core", "x"), 0, 0)
    grad_tokens = call(
        token_kernel,
        shape((8, 16, D), BF16),
        (tokens, cotangent, gain, own_grad, above_grad, left_grad, corner_grad),
        [pltpu.VMEM((8, 16, D), F32)],
        moved=1 << 20,
    )
    grad_out_weight, grad_gain, grad_bias_table = call(
        finish_kernel,
        [shape((16, D), F32), shape((1, D), F32), shape((HEADS, NBIAS), F32)],
        (finals,),
        moved=1 << 17,
    )
    return (grad_tokens, grad_qkv, grad_out_weight, grad_gain.reshape(D), grad_bias_table.T)


def solution(mesh):
    parts = Mesh(mesh.devices.reshape([n for _, n in PARTS]), [name for name, _ in PARTS])
    return jax.shard_map(
        local,
        mesh=parts,
        in_specs=(P(ROWS, COLS, None), P(ROWS, COLS, None), P(ROWS, COLS), P(), P(), P(), P(), P()),
        out_specs=(P(ROWS, COLS, None), P(ROWS, COLS), P(ROWS, None), P(), P()),
        check_vma=False,
    )
```

```python
import jax
import jax.numpy as jnp
from jax import lax
from jax.experimental import pallas as pl
from jax.experimental.pallas import tpu as pltpu
from jax.sharding import Mesh
from jax.sharding import PartitionSpec as P

D = 512
HEADS = 16
HEAD_DIM = 32
WIN = 8
SHIFT = 4
NBIAS = 225
AREA = WIN * WIN
TOKENS = 128
GROUP = 4
SCALE = HEAD_DIM ** (-0.5)
EPSILON = 1e-05

F32 = jnp.float32
BF16 = jnp.bfloat16

PARTS = (("y", 8), ("zh", 2), ("core", 2), ("x", 4), ("zl", 6))
ROWS = ("y", "zh", "core")
COLS = ("x", "zl")
NROWS = 32
NCOLS = 24

ANY_PARAMS = pltpu.CompilerParams(vmem_limit_bytes=48 * 1024 * 1024)


def dot(a, b):
    return lax.dot_general(a, b, (((1,), (0,)), ((), ())), preferred_element_type=F32)


def dot_nt(a, b):
    return lax.dot_general(a, b, (((1,), (1,)), ((), ())), preferred_element_type=F32)


def dot_tn(a, b):
    return lax.dot_general(a, b, (((0,), (0,)), ((), ())), preferred_element_type=F32)


def iota(shape, dim):
    return lax.broadcasted_iota(jnp.int32, shape, dim)


def split_high_low(value):
    high = value.astype(BF16)
    low = (value - high.astype(F32)).astype(BF16)
    return high, low


def layer_stats(floats):
    average = jnp.mean(floats, axis=-1, keepdims=True)
    centred = floats - average
    variance = jnp.mean(centred * centred, axis=-1, keepdims=True)
    inv_std = lax.rsqrt(variance + EPSILON)
    return centred * inv_std, inv_std


def pack_kernel(tok, cot, reg, to_up, to_left, to_diag, tok_v, cot_v, reg_v, sem):
    copies = [
        pltpu.make_async_copy(src, dst, sem.at[k])
        for k, (src, dst) in enumerate(((tok, tok_v), (cot, cot_v), (reg, reg_v)))
    ]
    for copy in copies:
        copy.start()
    to_up[96:112] = jnp.zeros((16, D), BF16)
    to_left[8] = jnp.zeros((4, D), BF16)
    to_diag[8] = jnp.zeros((4, D), BF16)
    for copy in copies:
        copy.wait()
    for k, src in ((0, tok_v), (4, cot_v)):
        for r in range(0, SHIFT, 2):
            first = src[r].astype(F32)
            second = src[r + 1].astype(F32)
            at = (k + r) * 12
            to_up[at : at + 24] = jnp.concatenate([first[4:16], second[4:16]], axis=0).astype(BF16)
        for r in range(SHIFT):
            to_diag[k + r] = src[r].astype(F32)[0:4].astype(BF16)
            to_left[k + r] = src[SHIFT + r].astype(F32)[0:4].astype(BF16)
    classes = reg_v[...].astype(F32)
    to_up[96:104, 0:16] = classes.astype(BF16)
    to_diag[8, 0:4, 0:16] = classes[0:4].astype(BF16)
    to_left[8, 0:4, 0:16] = classes[4:8].astype(BF16)


def bias_kernel(table_far, bucket_far, bias, bucket2, table, bucket, sem):
    copies = [
        pltpu.make_async_copy(table_far, table, sem.at[0]),
        pltpu.make_async_copy(bucket_far, bucket, sem.at[1]),
    ]
    for copy in copies:
        copy.start()
    for copy in copies:
        copy.wait()
    turned = jnp.concatenate([table[...], jnp.zeros((HEADS, 256 - NBIAS), F32)], axis=1)
    both = jnp.concatenate([bucket[...], bucket[...]], axis=1)
    bucket2[...] = jnp.where(iota((32, 128), 1) < 64, both[0:32], both[32:64])
    for block in range(AREA // 8):
        index = both[block * 8 : block * 8 + 8]
        upper = index >= 128
        within = jnp.bitwise_and(index, 127)
        for h in range(HEADS):
            first = jnp.broadcast_to(turned[h : h + 1, 0:128], (8, 128))
            second = jnp.broadcast_to(turned[h : h + 1, 128:256], (8, 128))
            got_first = jnp.take_along_axis(first, within, axis=1, mode="promise_in_bounds")
            got_second = jnp.take_along_axis(second, within, axis=1, mode="promise_in_bounds")
            bias[h, block * 8 : block * 8 + 8, :] = jnp.where(upper, got_second, got_first)


def window_kernel(
    tok_far, cot_far, reg_far, wqkv_far, wout_far, gain_far, bias, bucket2, up, left, diag,
    send, keep, own_grad, down_grad, right_grad, diag_grad,
    frame_t, frame_c, labels, packed, attended, grad_att, pairs, grad_in,
    tok, cot, reg, wqkv, wout, gain, sem,
):
    moves = (
        (tok_far, tok), (cot_far, cot), (reg_far, reg), (wqkv_far, wqkv),
        (wout_far, wout), (gain_far, gain),
    )
    copies = [pltpu.make_async_copy(src, dst, sem.at[k]) for k, (src, dst) in enumerate(moves)]
    for copy in copies:
        copy.start()
    for copy in copies[0:3]:
        copy.wait()

    up_f = up[...].astype(F32)
    for src, k, frame in ((tok, 0, frame_t), (cot, 4, frame_c)):
        for r in range(SHIFT):
            own = src[SHIFT + r].astype(F32)
            frame[r * 8 : r * 8 + 8, :] = own[4:12]
            frame[64 + r * 8 : 64 + r * 8 + 4, :] = own[12:16]
            frame[64 + r * 8 + 4 : 64 + r * 8 + 8, :] = left[k + r].astype(F32)
            s = SHIFT + r
            below = up_f[(k + r) * 12 : (k + r) * 12 + 12]
            frame[s * 8 : s * 8 + 8, :] = below[0:8]
            frame[64 + s * 8 : 64 + s * 8 + 4, :] = below[8:12]
            frame[64 + s * 8 + 4 : 64 + s * 8 + 8, :] = diag[k + r].astype(F32)

    mine = reg[...].astype(F32)
    labels[...] = jnp.zeros_like(labels)
    labels[0:4, 0:12] = mine[4:8, 4:16]
    labels[0:4, 12:16] = left[8, 0:4, 0:16].astype(F32)[:, 0:4]
    labels[4:8, 0:12] = up_f[96:100, 4:16]
    labels[4:8, 12:16] = diag[8, 0:4, 0:16].astype(F32)[:, 0:4]
    row_tile = (lax.axis_index("y") * 2 + lax.axis_index("zh")) * 2 + lax.axis_index("core")
    last = (row_tile == NROWS - 1).astype(F32)
    flags = jnp.where(iota((8, 128), 0) >= 4, 2.0, 0.0) * last
    coded = labels[...] + flags + jnp.where(iota((8, 128), 1) >= 8, 4.0, 0.0)
    token_lane = iota((128, 128), 1)
    token_row = iota((128, 128), 0)

    def column_of(token):
        return (token // 64) * 8 + token % 8

    def row_of(token):
        return (token // 8) % 8

    pick_lane = (column_of(token_lane) == token_row).astype(BF16)
    wide = dot(coded.astype(BF16), pick_lane)
    code_row = jnp.sum(
        jnp.where(row_of(iota((8, 128), 1)) == iota((8, 128), 0), wide, 0.0), axis=0, keepdims=True
    )
    pick_row = (column_of(token_row) == token_lane).astype(BF16)
    padded_codes = jnp.concatenate([coded, jnp.zeros((120, 128), F32)], axis=0).astype(BF16)
    tall = dot_nt(pick_row, padded_codes)
    code_col = jnp.sum(
        jnp.where(row_of(token_row) == token_lane, tall, 0.0), axis=1, keepdims=True
    )
    allowed = jnp.broadcast_to(code_col, (128, 128)) == jnp.broadcast_to(code_row, (128, 128))
    allowed4 = jnp.concatenate([allowed.astype(F32)] * GROUP, axis=0) > 0.5

    hat, _ = layer_stats(frame_t[...])
    copies[5].wait()
    normed = (hat * gain[...]).astype(BF16)
    cots = frame_c[...].astype(BF16)
    for copy in copies[3:5]:
        copy.wait()
    packed[...] = dot(normed, wqkv[...]).astype(BF16)
    grad_att[...] = dot_nt(cots, wout[...]).astype(BF16)
    send[0:TOKENS, 3 * D : 4 * D] = cots

    lane_head = iota((TOKENS, 128), 1) // HEAD_DIM
    masks = [lane_head == h for h in range(GROUP)]

    def stacked(value):
        return jnp.concatenate(
            [jnp.where(m, value, jnp.zeros_like(value)) for m in masks], axis=0
        )

    def beside(value):
        return jnp.concatenate([value[h * 128 : h * 128 + 128] for h in range(GROUP)], axis=1)

    for g in range(HEADS // GROUP):
        at = g * 128
        query = packed[:, at : at + 128]
        key = packed[:, D + at : D + at + 128]
        value = packed[:, 2 * D + at : 2 * D + at + 128]
        outer = grad_att[:, at : at + 128]
        query_s = stacked(query)
        outer_s = stacked(outer)
        biases = []
        for h in range(GROUP):
            one = bias[g * GROUP + h]
            biases += [one, one]
        scores = dot_nt(query_s, key) * SCALE + jnp.concatenate(biases, axis=0)
        scores = jnp.where(allowed4, scores, -1e30)
        raised = jnp.exp(scores - jnp.max(scores, axis=-1, keepdims=True))
        probs = raised / jnp.sum(raised, axis=-1, keepdims=True)
        probs_low = probs.astype(BF16)
        grad_probs = dot_nt(outer_s, value)
        inner = probs * grad_probs
        grad_scores = probs * (grad_probs - jnp.sum(inner, axis=-1, keepdims=True))
        grad_scaled = (grad_scores * SCALE).astype(BF16)
        attended[:, at : at + 128] = dot(beside(probs_low), stacked(value)).astype(BF16)
        send[0:TOKENS, at : at + 128] = dot(beside(grad_scaled), stacked(key)).astype(BF16)
        send[0:TOKENS, D + at : D + at + 128] = dot_tn(grad_scaled, query_s).astype(BF16)
        send[0:TOKENS, 2 * D + at : 2 * D + at + 128] = dot_tn(probs_low, outer_s).astype(BF16)
        for h in range(GROUP):
            one = grad_scores[h * 128 : h * 128 + 128]
            pairs[g * GROUP + h] = (one[0:32] + one[96:128]) + pltpu.roll(
                one[32:64] + one[64:96], 64, 1
            )

    core = lax.axis_index("core")
    for k, matrix in ((0, normed), (1, attended[...])):
        turned = matrix.astype(F32).T.reshape(16, 2, 16, TOKENS)
        even, odd = turned[:, 0].reshape(256, TOKENS), turned[:, 1].reshape(256, TOKENS)
        kept = jnp.where(core == 0, even, odd).astype(BF16)
        sent = jnp.where(core == 0, odd, even).astype(BF16)
        for b in range(2):
            lane = (2 * k + b) * 128
            keep[:, lane : lane + 128] = kept[b * 128 : b * 128 + 128]
            send[0:TOKENS, 4 * D + lane : 4 * D + lane + 128] = sent[b * 128 : b * 128 + 128]

    grad_normed = dot_nt(send[0:TOKENS, 0 : 3 * D], wqkv[...])
    grad_in[...] = grad_normed
    gain_sum = jnp.sum(grad_normed * hat, axis=0, keepdims=True)

    bucket_of = iota((256, 128), 0)
    step = 2

    def add_rows(k, total):
        parts, hots = [], []
        for t in range(step):
            i = k * step + t
            parts.append(pairs[:, i, :])
            which = jnp.broadcast_to(bucket2[pl.ds(i, 1), :], (256, 128))
            hots.append((bucket_of == which).astype(BF16))
        high, low = split_high_low(jnp.concatenate(parts, axis=1))
        both = jnp.concatenate([high, low], axis=0)
        return total + dot_nt(both, jnp.concatenate(hots, axis=1))

    sums = lax.fori_loop(
        0, AREA // 2 // step, add_rows, jnp.zeros((2 * HEADS, 256), F32), unroll=True
    )
    table = sums[0:HEADS] + sums[HEADS : 2 * HEADS]
    high, low = split_high_low(table)
    send[TOKENS : TOKENS + 16, 0:256] = high
    send[TOKENS : TOKENS + 16, 256:512] = low
    high, low = split_high_low(jnp.concatenate([gain_sum, jnp.zeros((15, D), F32)], axis=0))
    send[TOKENS : TOKENS + 16, 512:1024] = high
    send[TOKENS : TOKENS + 16, 1024:1536] = low
    send[TOKENS : TOKENS + 16, 1536:2560] = jnp.zeros((16, 1024), BF16)

    for r in range(SHIFT):
        s = SHIFT + r
        own_grad[r, 0:8, :] = grad_in[r * 8 : r * 8 + 8, :]
        own_grad[r, 8:12, :] = grad_in[64 + r * 8 : 64 + r * 8 + 4, :]
        right_grad[r] = grad_in[64 + r * 8 : 64 + r * 8 + 8, :][4:8].astype(BF16)
        down_grad[r] = jnp.concatenate(
            [grad_in[s * 8 : s * 8 + 8, :], grad_in[64 + s * 8 : 64 + s * 8 + 8, :][0:4]], axis=0
        ).astype(BF16)
        diag_grad[r] = grad_in[64 + s * 8 : 64 + s * 8 + 8, :][4:8].astype(BF16)


def product_kernel(mine, other, keep, out):
    def rows(block):
        lane = block * 128
        return jnp.concatenate(
            [keep[:, lane : lane + 128], other[0:TOKENS, 4 * D + lane : 4 * D + lane + 128]], axis=1
        )

    right = jnp.concatenate([mine[0:TOKENS, 0 : 4 * D], other[0:TOKENS, 0 : 4 * D]], axis=0)
    for half in range(2):
        qkv = dot(rows(half), right[:, 0 : 3 * D]).astype(BF16)
        proj = dot(rows(2 + half), right[:, 3 * D : 4 * D]).astype(BF16)
        for k in range(4):
            for x in range(4):
                to = x * 8 + half * 4 + k
                at = k * 32
                for block in range(3):
                    lane = x * 384 + block * 128
                    out[to, block * 32 : block * 32 + 32, :] = qkv[at : at + 32, lane : lane + 128]
                out[to, 96:128, :] = proj[at : at + 32, x * 128 : x * 128 + 128]
    first = lax.axis_index("core") == 0
    small = mine[TOKENS : TOKENS + 16, 0:1536].astype(F32) + other[TOKENS : TOKENS + 16, 0:1536].astype(F32)
    table = small[:, 0:256] + small[:, 256:512]
    table = jnp.where(first, table[0:8], table[8:16])
    gain = small[0:8, 512:1024] + small[0:8, 1024:1536]
    gain = jnp.where(first, gain[:, 0:256], gain[:, 256:512])
    for x in range(4):
        lane = (x // 2) * 128
        piece = gain[:, lane : lane + 128]
        if x % 2 == 1:
            piece = pltpu.roll(piece, 64, 1)
        part = jnp.concatenate(
            [table[2 * x : 2 * x + 2, 0:128], table[2 * x : 2 * x + 2, 128:256], piece[0:4]], axis=0
        ).astype(BF16)
        for y in range(8):
            out[x * 8 + y, 128:136, :] = part


def plane_sum_kernel(parts, out):
    total = jnp.sum(parts[...].astype(F32), axis=0)
    left_half = iota((8, 128), 1) < 64
    small = total[128:136]
    for zh in range(2):
        proj = total[96 + zh * 16 : 112 + zh * 16].astype(BF16)
        for zl in range(6):
            at = (zl // 2) * 32 + zh * 16
            upper, lower = total[at : at + 8], total[at + 8 : at + 16]
            if zl % 2 == 0:
                lower = pltpu.roll(lower, 64, 1)
            else:
                upper = pltpu.roll(upper, 64, 1)
            qkv = jnp.where(left_half, upper, lower)
            out[zh * 6 + zl, 0:16, :] = proj
            out[zh * 6 + zl, 16:32, :] = jnp.concatenate([qkv, small], axis=0).astype(BF16)


def line_sum_kernel(parts, qkv, out):
    total = jnp.sum(parts[...].astype(F32), axis=0)
    qkv[0:8, :] = total[16:24, 0:64]
    qkv[8:16, :] = pltpu.roll(total[16:24], 64, 1)[:, 0:64]
    for to in range(8):
        out[to, 0:16, :] = total[0:16]
        out[to, 16:24, :] = total[24:32]


def finish_kernel(parts, proj, gain, table):
    core = lax.axis_index("core")
    for x in range(4):
        proj[:, x * 128 : x * 128 + 128] = parts[core * 4 + x, 0:16, :]
    left_half = iota((1, 128), 1) < 64
    low, high = [], []
    for k in range(8):
        low.append(parts[k, 16:18, :])
        high.append(parts[k, 18:20, :])
    for k in range(4):
        second = pltpu.roll(parts[2 * k + 1, 16:24, :], 64, 1)[4:5]
        gain[:, k * 128 : k * 128 + 128] = jnp.where(left_half, parts[2 * k, 20:21, :], second)
    table[:, 0:128] = jnp.concatenate(low, axis=0)
    table[:, 128:NBIAS] = jnp.concatenate(high, axis=0)[:, 0 : NBIAS - 128]


def token_kernel(tok, cot, gain, own, above, left, diag, out, grads):
    for r in range(SHIFT):
        grads[r, 0:4, :] = diag[r].astype(F32)
        grads[r, 4:16, :] = above[r].astype(F32)
        grads[SHIFT + r, 0:4, :] = left[r].astype(F32)
        grads[SHIFT + r, 4:16, :] = own[r]
    hat, inv_std = layer_stats(tok[...].astype(F32))
    grad_hat = grads[...] * gain[...].reshape(1, 1, D)
    moved = (
        grad_hat
        - jnp.mean(grad_hat, axis=-1, keepdims=True)
        - hat * jnp.mean(grad_hat * hat, axis=-1, keepdims=True)
    )
    out[...] = (cot[...].astype(F32) + inv_std * moved).astype(BF16)


def shape(dims, dtype):
    return jax.ShapeDtypeStruct(dims, dtype)


def call(kernel, outs, args, scratch=(), flops=0, moved=0, remain=(), params=ANY_PARAMS):
    args = [
        pltpu.with_memory_space_constraint(arg, pltpu.HBM) if k in remain else arg
        for k, arg in enumerate(args)
    ]
    return pl.pallas_call(
        kernel,
        in_specs=[
            pl.BlockSpec(memory_space=pltpu.HBM if k in remain else pltpu.VMEM)
            for k in range(len(args))
        ],
        out_shape=outs,
        scratch_shapes=list(scratch),
        compiler_params=params,
        cost_estimate=pl.CostEstimate(flops=flops, bytes_accessed=moved, transcendentals=0),
    )(*args)


def neighbour(value, down, right):
    pairs = [
        (r * NCOLS + c, ((r + down) % NROWS) * NCOLS + (c + right) % NCOLS)
        for r in range(NROWS)
        for c in range(NCOLS)
    ]
    return lax.ppermute(value, ROWS + COLS, pairs)


def local(tokens, cotangent, region, norm_gain, qkv_weight, out_weight, bias_table, bias_bucket):
    gain = norm_gain.reshape(1, D)
    to_up, to_left, to_diag = call(
        pack_kernel,
        [shape((112, D), BF16), shape((9, 4, D), BF16), shape((9, 4, D), BF16)],
        (tokens, cotangent, region),
        [
            pltpu.VMEM((8, 16, D), BF16),
            pltpu.VMEM((8, 16, D), BF16),
            pltpu.VMEM((8, 16), jnp.int32),
            pltpu.SemaphoreType.DMA((3,)),
        ],
        moved=1 << 19,
        remain=(0, 1, 2),
    )
    up = neighbour(to_up, -1, 0)
    left = neighbour(to_left, 0, -1)
    diag = neighbour(to_diag, -1, -1)
    bias, bucket2 = call(
        bias_kernel,
        [
            shape((HEADS, AREA, 128), F32),
            shape((AREA // 2, 128), jnp.int32),
        ],
        (bias_table.T, bias_bucket),
        [
            pltpu.VMEM((HEADS, NBIAS), F32),
            pltpu.VMEM((AREA, AREA), jnp.int32),
            pltpu.SemaphoreType.DMA((2,)),
        ],
        moved=1 << 23,
        remain=(0, 1),
    )
    send, keep, own_grad, down_grad, right_grad, diag_grad = call(
        window_kernel,
        [
            shape((TOKENS + 16, 5 * D), BF16),
            shape((TOKENS, D), BF16),
            shape((4, 12, D), F32),
            shape((4, 12, D), BF16),
            shape((4, 4, D), BF16),
            shape((4, 4, D), BF16),
        ],
        (tokens, cotangent, region, qkv_weight, out_weight, gain, bias, bucket2, up, left, diag),
        [
            pltpu.VMEM((TOKENS, D), F32),
            pltpu.VMEM((TOKENS, D), F32),
            pltpu.VMEM((8, 128), F32),
            pltpu.VMEM((TOKENS, 3 * D), BF16),
            pltpu.VMEM((TOKENS, D), BF16),
            pltpu.VMEM((TOKENS, D), BF16),
            pltpu.VMEM((HEADS, AREA // 2, 128), F32),
            pltpu.VMEM((TOKENS, D), F32),
            pltpu.VMEM((8, 16, D), BF16),
            pltpu.VMEM((8, 16, D), BF16),
            pltpu.VMEM((8, 16), jnp.int32),
            pltpu.VMEM((D, 3 * D), BF16),
            pltpu.VMEM((D, D), BF16),
            pltpu.VMEM((1, D), F32),
            pltpu.SemaphoreType.DMA((6,)),
        ],
        flops=1 << 30,
        moved=1 << 23,
        remain=tuple(range(6)),
    )
    other = lax.ppermute(send, "core", [(0, 1), (1, 0)])
    products = call(
        product_kernel,
        shape((32, 136, 128), BF16),
        (send, other, keep),
        flops=1 << 29,
        moved=1 << 21,
    )
    products, down_grad, right_grad, diag_grad = lax.optimization_barrier(
        (products, down_grad, right_grad, diag_grad)
    )
    planes = lax.all_to_all(products, ("x", "y"), 0, 0)
    above_grad = neighbour(down_grad, 1, 0)
    left_grad = neighbour(right_grad, 0, 1)
    corner_grad = neighbour(diag_grad, 1, 1)
    chunks = call(plane_sum_kernel, shape((12, 32, 128), BF16), (planes,), moved=1 << 21)
    chunks, above_grad, left_grad, corner_grad = lax.optimization_barrier(
        (chunks, above_grad, left_grad, corner_grad)
    )
    lines = lax.all_to_all(chunks, ("zh", "zl"), 0, 0)
    grad_qkv, finals = call(
        line_sum_kernel, [shape((16, 64), F32), shape((8, 24, 128), F32)], (lines,), moved=1 << 18
    )
    finals = lax.all_to_all(finals, ("core", "x"), 0, 0)
    grad_tokens = call(
        token_kernel,
        shape((8, 16, D), BF16),
        (tokens, cotangent, gain, own_grad, above_grad, left_grad, corner_grad),
        [pltpu.VMEM((8, 16, D), F32)],
        moved=1 << 20,
    )
    grad_out_weight, grad_gain, grad_bias_table = call(
        finish_kernel,
        [shape((16, D), F32), shape((1, D), F32), shape((HEADS, NBIAS), F32)],
        (finals,),
        moved=1 << 17,
    )
    return (grad_tokens, grad_qkv, grad_out_weight, grad_gain.reshape(D), grad_bias_table.T)


def solution(mesh):
    parts = Mesh(mesh.devices.reshape([n for _, n in PARTS]), [name for name, _ in PARTS])
    return jax.shard_map(
        local,
        mesh=parts,
        in_specs=(P(ROWS, COLS, None), P(ROWS, COLS, None), P(ROWS, COLS), P(), P(), P(), P(), P()),
        out_specs=(P(ROWS, COLS, None), P(ROWS, COLS), P(ROWS, None), P(), P()),
        check_vma=False,
    )
```

```python
import jax
import jax.numpy as jnp
from jax import lax
from jax.experimental import pallas as pl
from jax.experimental.pallas import tpu as pltpu
from jax.sharding import Mesh
from jax.sharding import PartitionSpec as P

D = 512
HEADS = 16
HEAD_DIM = 32
WIN = 8
SHIFT = 4
NBIAS = 225
AREA = WIN * WIN
TOKENS = 128
GROUP = 4
SCALE = HEAD_DIM ** (-0.5)
EPSILON = 1e-05

F32 = jnp.float32
BF16 = jnp.bfloat16

PARTS = (("y", 8), ("zh", 2), ("core", 2), ("x", 4), ("zl", 6))
ROWS = ("y", "zh", "core")
COLS = ("x", "zl")
NROWS = 32
NCOLS = 24

ANY_PARAMS = pltpu.CompilerParams(vmem_limit_bytes=48 * 1024 * 1024)


def dot(a, b):
    return lax.dot_general(a, b, (((1,), (0,)), ((), ())), preferred_element_type=F32)


def dot_nt(a, b):
    return lax.dot_general(a, b, (((1,), (1,)), ((), ())), preferred_element_type=F32)


def dot_tn(a, b):
    return lax.dot_general(a, b, (((0,), (0,)), ((), ())), preferred_element_type=F32)


def iota(shape, dim):
    return lax.broadcasted_iota(jnp.int32, shape, dim)


def split_high_low(value):
    high = value.astype(BF16)
    low = (value - high.astype(F32)).astype(BF16)
    return high, low


def layer_stats(floats):
    average = jnp.mean(floats, axis=-1, keepdims=True)
    centred = floats - average
    variance = jnp.mean(centred * centred, axis=-1, keepdims=True)
    inv_std = lax.rsqrt(variance + EPSILON)
    return centred * inv_std, inv_std


def pack_kernel(tok, cot, reg, to_up, to_left, to_diag, tok_v, cot_v, reg_v, sem):
    copies = [
        pltpu.make_async_copy(src, dst, sem.at[k])
        for k, (src, dst) in enumerate(((tok, tok_v), (cot, cot_v), (reg, reg_v)))
    ]
    for copy in copies:
        copy.start()
    to_up[96:112] = jnp.zeros((16, D), BF16)
    to_left[8] = jnp.zeros((4, D), BF16)
    to_diag[8] = jnp.zeros((4, D), BF16)
    for copy in copies:
        copy.wait()
    for k, src in ((0, tok_v), (4, cot_v)):
        for r in range(0, SHIFT, 2):
            first = src[r].astype(F32)
            second = src[r + 1].astype(F32)
            at = (k + r) * 12
            to_up[at : at + 24] = jnp.concatenate([first[4:16], second[4:16]], axis=0).astype(BF16)
        for r in range(SHIFT):
            to_diag[k + r] = src[r].astype(F32)[0:4].astype(BF16)
            to_left[k + r] = src[SHIFT + r].astype(F32)[0:4].astype(BF16)
    classes = reg_v[...].astype(F32)
    to_up[96:104, 0:16] = classes.astype(BF16)
    to_diag[8, 0:4, 0:16] = classes[0:4].astype(BF16)
    to_left[8, 0:4, 0:16] = classes[4:8].astype(BF16)


def bias_kernel(table_far, bucket_far, bias, bucket2, table, bucket, sem):
    copies = [
        pltpu.make_async_copy(table_far, table, sem.at[0]),
        pltpu.make_async_copy(bucket_far, bucket, sem.at[1]),
    ]
    for copy in copies:
        copy.start()
    for copy in copies:
        copy.wait()
    turned = jnp.concatenate([table[...], jnp.zeros((HEADS, 256 - NBIAS), F32)], axis=1)
    both = jnp.concatenate([bucket[...], bucket[...]], axis=1)
    bucket2[...] = jnp.where(iota((32, 128), 1) < 64, both[0:32], both[32:64])
    for block in range(AREA // 8):
        index = both[block * 8 : block * 8 + 8]
        upper = index >= 128
        within = jnp.bitwise_and(index, 127)
        for h in range(HEADS):
            first = jnp.broadcast_to(turned[h : h + 1, 0:128], (8, 128))
            second = jnp.broadcast_to(turned[h : h + 1, 128:256], (8, 128))
            got_first = jnp.take_along_axis(first, within, axis=1, mode="promise_in_bounds")
            got_second = jnp.take_along_axis(second, within, axis=1, mode="promise_in_bounds")
            bias[h, block * 8 : block * 8 + 8, :] = jnp.where(upper, got_second, got_first)


def window_kernel(
    tok_far, cot_far, reg_far, wqkv_far, wout_far, gain_far, bias, bucket2, up, diag, left,
    send, keep, own_grad, down_grad, right_grad, diag_grad,
    frame_t, frame_c, labels, packed, attended, grad_att, pairs, grad_in,
    tok, cot, reg, wqkv, wout, gain, sem,
):
    moves = (
        (tok_far, tok), (cot_far, cot), (reg_far, reg), (wqkv_far, wqkv),
        (wout_far, wout), (gain_far, gain),
    )
    copies = [pltpu.make_async_copy(src, dst, sem.at[k]) for k, (src, dst) in enumerate(moves)]
    for copy in copies:
        copy.start()
    for copy in copies[0:3]:
        copy.wait()

    up_f = up[...].astype(F32)
    for src, k, frame in ((tok, 0, frame_t), (cot, 4, frame_c)):
        for r in range(SHIFT):
            own = src[SHIFT + r].astype(F32)
            frame[r * 8 : r * 8 + 8, :] = own[4:12]
            frame[64 + r * 8 : 64 + r * 8 + 4, :] = own[12:16]
            frame[64 + r * 8 + 4 : 64 + r * 8 + 8, :] = left[k + r].astype(F32)
            s = SHIFT + r
            below = up_f[(k + r) * 12 : (k + r) * 12 + 12]
            frame[s * 8 : s * 8 + 8, :] = below[0:8]
            frame[64 + s * 8 : 64 + s * 8 + 4, :] = below[8:12]
            frame[64 + s * 8 + 4 : 64 + s * 8 + 8, :] = diag[k + r].astype(F32)

    mine = reg[...].astype(F32)
    labels[...] = jnp.zeros_like(labels)
    labels[0:4, 0:12] = mine[4:8, 4:16]
    labels[0:4, 12:16] = left[8, 0:4, 0:16].astype(F32)[:, 0:4]
    labels[4:8, 0:12] = up_f[96:100, 4:16]
    labels[4:8, 12:16] = diag[8, 0:4, 0:16].astype(F32)[:, 0:4]
    row_tile = (lax.axis_index("y") * 2 + lax.axis_index("zh")) * 2 + lax.axis_index("core")
    last = (row_tile == NROWS - 1).astype(F32)
    flags = jnp.where(iota((8, 128), 0) >= 4, 2.0, 0.0) * last
    coded = labels[...] + flags + jnp.where(iota((8, 128), 1) >= 8, 4.0, 0.0)
    token_lane = iota((128, 128), 1)
    token_row = iota((128, 128), 0)

    def column_of(token):
        return (token // 64) * 8 + token % 8

    def row_of(token):
        return (token // 8) % 8

    pick_lane = (column_of(token_lane) == token_row).astype(BF16)
    wide = dot(coded.astype(BF16), pick_lane)
    code_row = jnp.sum(
        jnp.where(row_of(iota((8, 128), 1)) == iota((8, 128), 0), wide, 0.0), axis=0, keepdims=True
    )
    pick_row = (column_of(token_row) == token_lane).astype(BF16)
    padded_codes = jnp.concatenate([coded, jnp.zeros((120, 128), F32)], axis=0).astype(BF16)
    tall = dot_nt(pick_row, padded_codes)
    code_col = jnp.sum(
        jnp.where(row_of(token_row) == token_lane, tall, 0.0), axis=1, keepdims=True
    )
    allowed = jnp.broadcast_to(code_col, (128, 128)) == jnp.broadcast_to(code_row, (128, 128))
    allowed4 = jnp.concatenate([allowed.astype(F32)] * GROUP, axis=0) > 0.5

    hat, _ = layer_stats(frame_t[...])
    copies[5].wait()
    normed = (hat * gain[...]).astype(BF16)
    cots = frame_c[...].astype(BF16)
    for copy in copies[3:5]:
        copy.wait()
    packed[...] = dot(normed, wqkv[...]).astype(BF16)
    grad_att[...] = dot_nt(cots, wout[...]).astype(BF16)
    send[0:TOKENS, 3 * D : 4 * D] = cots

    lane_head = iota((TOKENS, 128), 1) // HEAD_DIM
    masks = [lane_head == h for h in range(GROUP)]

    def stacked(value):
        return jnp.concatenate(
            [jnp.where(m, value, jnp.zeros_like(value)) for m in masks], axis=0
        )

    def beside(value):
        return jnp.concatenate([value[h * 128 : h * 128 + 128] for h in range(GROUP)], axis=1)

    for g in range(HEADS // GROUP):
        at = g * 128
        query = packed[:, at : at + 128]
        key = packed[:, D + at : D + at + 128]
        value = packed[:, 2 * D + at : 2 * D + at + 128]
        outer = grad_att[:, at : at + 128]
        query_s = stacked(query)
        outer_s = stacked(outer)
        biases = []
        for h in range(GROUP):
            one = bias[g * GROUP + h]
            biases += [one, one]
        scores = dot_nt(query_s, key) * SCALE + jnp.concatenate(biases, axis=0)
        scores = jnp.where(allowed4, scores, -1e30)
        raised = jnp.exp(scores - jnp.max(scores, axis=-1, keepdims=True))
        probs = raised / jnp.sum(raised, axis=-1, keepdims=True)
        probs_low = probs.astype(BF16)
        grad_probs = dot_nt(outer_s, value)
        inner = probs * grad_probs
        grad_scores = probs * (grad_probs - jnp.sum(inner, axis=-1, keepdims=True))
        grad_scaled = (grad_scores * SCALE).astype(BF16)
        attended[:, at : at + 128] = dot(beside(probs_low), stacked(value)).astype(BF16)
        send[0:TOKENS, at : at + 128] = dot(beside(grad_scaled), stacked(key)).astype(BF16)
        send[0:TOKENS, D + at : D + at + 128] = dot_tn(grad_scaled, query_s).astype(BF16)
        send[0:TOKENS, 2 * D + at : 2 * D + at + 128] = dot_tn(probs_low, outer_s).astype(BF16)
        for h in range(GROUP):
            one = grad_scores[h * 128 : h * 128 + 128]
            pairs[g * GROUP + h] = (one[0:32] + one[96:128]) + pltpu.roll(
                one[32:64] + one[64:96], 64, 1
            )

    core = lax.axis_index("core")
    for k, matrix in ((0, normed), (1, attended[...])):
        turned = matrix.astype(F32).T.reshape(16, 2, 16, TOKENS)
        even, odd = turned[:, 0].reshape(256, TOKENS), turned[:, 1].reshape(256, TOKENS)
        kept = jnp.where(core == 0, even, odd).astype(BF16)
        sent = jnp.where(core == 0, odd, even).astype(BF16)
        for b in range(2):
            lane = (2 * k + b) * 128
            keep[:, lane : lane + 128] = kept[b * 128 : b * 128 + 128]
            send[0:TOKENS, 4 * D + lane : 4 * D + lane + 128] = sent[b * 128 : b * 128 + 128]

    grad_normed = dot_nt(send[0:TOKENS, 0 : 3 * D], wqkv[...])
    grad_in[...] = grad_normed
    gain_sum = jnp.sum(grad_normed * hat, axis=0, keepdims=True)

    bucket_of = iota((256, 128), 0)
    step = 2

    def add_rows(k, total):
        parts, hots = [], []
        for t in range(step):
            i = k * step + t
            parts.append(pairs[:, i, :])
            which = jnp.broadcast_to(bucket2[pl.ds(i, 1), :], (256, 128))
            hots.append((bucket_of == which).astype(BF16))
        high, low = split_high_low(jnp.concatenate(parts, axis=1))
        both = jnp.concatenate([high, low], axis=0)
        return total + dot_nt(both, jnp.concatenate(hots, axis=1))

    sums = lax.fori_loop(
        0, AREA // 2 // step, add_rows, jnp.zeros((2 * HEADS, 256), F32), unroll=True
    )
    table = sums[0:HEADS] + sums[HEADS : 2 * HEADS]
    high, low = split_high_low(table)
    send[TOKENS : TOKENS + 16, 0:256] = high
    send[TOKENS : TOKENS + 16, 256:512] = low
    high, low = split_high_low(jnp.concatenate([gain_sum, jnp.zeros((15, D), F32)], axis=0))
    send[TOKENS : TOKENS + 16, 512:1024] = high
    send[TOKENS : TOKENS + 16, 1024:1536] = low
    send[TOKENS : TOKENS + 16, 1536:2560] = jnp.zeros((16, 1024), BF16)

    for r in range(SHIFT):
        s = SHIFT + r
        own_grad[r, 0:8, :] = grad_in[r * 8 : r * 8 + 8, :]
        own_grad[r, 8:12, :] = grad_in[64 + r * 8 : 64 + r * 8 + 4, :]
        right_grad[r] = grad_in[64 + r * 8 : 64 + r * 8 + 8, :][4:8].astype(BF16)
        down_grad[r] = jnp.concatenate(
            [grad_in[s * 8 : s * 8 + 8, :], grad_in[64 + s * 8 : 64 + s * 8 + 8, :][0:4]], axis=0
        ).astype(BF16)
        diag_grad[r] = grad_in[64 + s * 8 : 64 + s * 8 + 8, :][4:8].astype(BF16)


def product_kernel(mine, other, keep, out):
    def rows(block):
        lane = block * 128
        return jnp.concatenate(
            [keep[:, lane : lane + 128], other[0:TOKENS, 4 * D + lane : 4 * D + lane + 128]], axis=1
        )

    right = jnp.concatenate([mine[0:TOKENS, 0 : 4 * D], other[0:TOKENS, 0 : 4 * D]], axis=0)
    for half in range(2):
        qkv = dot(rows(half), right[:, 0 : 3 * D]).astype(BF16)
        proj = dot(rows(2 + half), right[:, 3 * D : 4 * D]).astype(BF16)
        for k in range(4):
            for x in range(4):
                to = x * 8 + half * 4 + k
                at = k * 32
                for block in range(3):
                    lane = x * 384 + block * 128
                    out[to, block * 32 : block * 32 + 32, :] = qkv[at : at + 32, lane : lane + 128]
                out[to, 96:128, :] = proj[at : at + 32, x * 128 : x * 128 + 128]
    first = lax.axis_index("core") == 0
    small = mine[TOKENS : TOKENS + 16, 0:1536].astype(F32) + other[TOKENS : TOKENS + 16, 0:1536].astype(F32)
    table = small[:, 0:256] + small[:, 256:512]
    table = jnp.where(first, table[0:8], table[8:16])
    gain = small[0:8, 512:1024] + small[0:8, 1024:1536]
    gain = jnp.where(first, gain[:, 0:256], gain[:, 256:512])
    for x in range(4):
        lane = (x // 2) * 128
        piece = gain[:, lane : lane + 128]
        if x % 2 == 1:
            piece = pltpu.roll(piece, 64, 1)
        part = jnp.concatenate(
            [table[2 * x : 2 * x + 2, 0:128], table[2 * x : 2 * x + 2, 128:256], piece[0:4]], axis=0
        ).astype(BF16)
        for y in range(8):
            out[x * 8 + y, 128:136, :] = part


def plane_sum_kernel(parts, out):
    total = jnp.sum(parts[...].astype(F32), axis=0)
    left_half = iota((8, 128), 1) < 64
    small = total[128:136]
    for zh in range(2):
        proj = total[96 + zh * 16 : 112 + zh * 16].astype(BF16)
        for zl in range(6):
            at = (zl // 2) * 32 + zh * 16
            upper, lower = total[at : at + 8], total[at + 8 : at + 16]
            if zl % 2 == 0:
                lower = pltpu.roll(lower, 64, 1)
            else:
                upper = pltpu.roll(upper, 64, 1)
            qkv = jnp.where(left_half, upper, lower)
            out[zh * 6 + zl, 0:16, :] = proj
            out[zh * 6 + zl, 16:32, :] = jnp.concatenate([qkv, small], axis=0).astype(BF16)


def line_sum_kernel(parts, qkv, out):
    total = jnp.sum(parts[...].astype(F32), axis=0)
    qkv[0:8, :] = total[16:24, 0:64]
    qkv[8:16, :] = pltpu.roll(total[16:24], 64, 1)[:, 0:64]
    for to in range(8):
        out[to, 0:16, :] = total[0:16]
        out[to, 16:24, :] = total[24:32]


def finish_kernel(parts, proj, gain, table):
    core = lax.axis_index("core")
    for x in range(4):
        proj[:, x * 128 : x * 128 + 128] = parts[core * 4 + x, 0:16, :]
    left_half = iota((1, 128), 1) < 64
    low, high = [], []
    for k in range(8):
        low.append(parts[k, 16:18, :])
        high.append(parts[k, 18:20, :])
    for k in range(4):
        second = pltpu.roll(parts[2 * k + 1, 16:24, :], 64, 1)[4:5]
        gain[:, k * 128 : k * 128 + 128] = jnp.where(left_half, parts[2 * k, 20:21, :], second)
    table[:, 0:128] = jnp.concatenate(low, axis=0)
    table[:, 128:NBIAS] = jnp.concatenate(high, axis=0)[:, 0 : NBIAS - 128]


def token_kernel(tok, cot, gain, own, above, left, diag, out, grads):
    for r in range(SHIFT):
        grads[r, 0:4, :] = diag[r].astype(F32)
        grads[r, 4:16, :] = above[r].astype(F32)
        grads[SHIFT + r, 0:4, :] = left[r].astype(F32)
        grads[SHIFT + r, 4:16, :] = own[r]
    hat, inv_std = layer_stats(tok[...].astype(F32))
    grad_hat = grads[...] * gain[...].reshape(1, 1, D)
    moved = (
        grad_hat
        - jnp.mean(grad_hat, axis=-1, keepdims=True)
        - hat * jnp.mean(grad_hat * hat, axis=-1, keepdims=True)
    )
    out[...] = (cot[...].astype(F32) + inv_std * moved).astype(BF16)


def shape(dims, dtype):
    return jax.ShapeDtypeStruct(dims, dtype)


def call(kernel, outs, args, scratch=(), flops=0, moved=0, remain=(), params=ANY_PARAMS):
    args = [
        pltpu.with_memory_space_constraint(arg, pltpu.HBM) if k in remain else arg
        for k, arg in enumerate(args)
    ]
    return pl.pallas_call(
        kernel,
        in_specs=[
            pl.BlockSpec(memory_space=pltpu.HBM if k in remain else pltpu.VMEM)
            for k in range(len(args))
        ],
        out_shape=outs,
        scratch_shapes=list(scratch),
        compiler_params=params,
        cost_estimate=pl.CostEstimate(flops=flops, bytes_accessed=moved, transcendentals=0),
    )(*args)


def neighbour(value, down, right):
    pairs = [
        (r * NCOLS + c, ((r + down) % NROWS) * NCOLS + (c + right) % NCOLS)
        for r in range(NROWS)
        for c in range(NCOLS)
    ]
    return lax.ppermute(value, ROWS + COLS, pairs)


def local(tokens, cotangent, region, norm_gain, qkv_weight, out_weight, bias_table, bias_bucket):
    gain = norm_gain.reshape(1, D)
    to_up, to_left, to_diag = call(
        pack_kernel,
        [shape((112, D), BF16), shape((9, 4, D), BF16), shape((9, 4, D), BF16)],
        (tokens, cotangent, region),
        [
            pltpu.VMEM((8, 16, D), BF16),
            pltpu.VMEM((8, 16, D), BF16),
            pltpu.VMEM((8, 16), jnp.int32),
            pltpu.SemaphoreType.DMA((3,)),
        ],
        moved=1 << 19,
        remain=(0, 1, 2),
    )
    up = neighbour(to_up, -1, 0)
    left = neighbour(to_left, 0, -1)
    diag = neighbour(to_diag, -1, -1)
    bias, bucket2 = call(
        bias_kernel,
        [
            shape((HEADS, AREA, 128), F32),
            shape((AREA // 2, 128), jnp.int32),
        ],
        (bias_table.T, bias_bucket),
        [
            pltpu.VMEM((HEADS, NBIAS), F32),
            pltpu.VMEM((AREA, AREA), jnp.int32),
            pltpu.SemaphoreType.DMA((2,)),
        ],
        moved=1 << 23,
        remain=(0, 1),
    )
    send, keep, own_grad, down_grad, right_grad, diag_grad = call(
        window_kernel,
        [
            shape((TOKENS + 16, 5 * D), BF16),
            shape((TOKENS, D), BF16),
            shape((4, 12, D), F32),
            shape((4, 12, D), BF16),
            shape((4, 4, D), BF16),
            shape((4, 4, D), BF16),
        ],
        (tokens, cotangent, region, qkv_weight, out_weight, gain, bias, bucket2, up, diag, left),
        [
            pltpu.VMEM((TOKENS, D), F32),
            pltpu.VMEM((TOKENS, D), F32),
            pltpu.VMEM((8, 128), F32),
            pltpu.VMEM((TOKENS, 3 * D), BF16),
            pltpu.VMEM((TOKENS, D), BF16),
            pltpu.VMEM((TOKENS, D), BF16),
            pltpu.VMEM((HEADS, AREA // 2, 128), F32),
            pltpu.VMEM((TOKENS, D), F32),
            pltpu.VMEM((8, 16, D), BF16),
            pltpu.VMEM((8, 16, D), BF16),
            pltpu.VMEM((8, 16), jnp.int32),
            pltpu.VMEM((D, 3 * D), BF16),
            pltpu.VMEM((D, D), BF16),
            pltpu.VMEM((1, D), F32),
            pltpu.SemaphoreType.DMA((6,)),
        ],
        flops=1 << 30,
        moved=1 << 23,
        remain=tuple(range(6)),
    )
    other = lax.ppermute(send, "core", [(0, 1), (1, 0)])
    products = call(
        product_kernel,
        shape((32, 136, 128), BF16),
        (send, other, keep),
        flops=1 << 29,
        moved=1 << 21,
    )
    products, down_grad, right_grad, diag_grad = lax.optimization_barrier(
        (products, down_grad, right_grad, diag_grad)
    )
    planes = lax.all_to_all(products, ("x", "y"), 0, 0)
    above_grad = neighbour(down_grad, 1, 0)
    left_grad = neighbour(right_grad, 0, 1)
    corner_grad = neighbour(diag_grad, 1, 1)
    chunks = call(plane_sum_kernel, shape((12, 32, 128), BF16), (planes,), moved=1 << 21)
    chunks, above_grad, left_grad, corner_grad = lax.optimization_barrier(
        (chunks, above_grad, left_grad, corner_grad)
    )
    lines = lax.all_to_all(chunks, ("zh", "zl"), 0, 0)
    grad_qkv, finals = call(
        line_sum_kernel, [shape((16, 64), F32), shape((8, 24, 128), F32)], (lines,), moved=1 << 18
    )
    finals = lax.all_to_all(finals, ("core", "x"), 0, 0)
    grad_tokens = call(
        token_kernel,
        shape((8, 16, D), BF16),
        (tokens, cotangent, gain, own_grad, above_grad, left_grad, corner_grad),
        [pltpu.VMEM((8, 16, D), F32)],
        moved=1 << 20,
    )
    grad_out_weight, grad_gain, grad_bias_table = call(
        finish_kernel,
        [shape((16, D), F32), shape((1, D), F32), shape((HEADS, NBIAS), F32)],
        (finals,),
        moved=1 << 17,
    )
    return (grad_tokens, grad_qkv, grad_out_weight, grad_gain.reshape(D), grad_bias_table.T)


def solution(mesh):
    parts = Mesh(mesh.devices.reshape([n for _, n in PARTS]), [name for name, _ in PARTS])
    return jax.shard_map(
        local,
        mesh=parts,
        in_specs=(P(ROWS, COLS, None), P(ROWS, COLS, None), P(ROWS, COLS), P(), P(), P(), P(), P()),
        out_specs=(P(ROWS, COLS, None), P(ROWS, COLS), P(ROWS, None), P(), P()),
        check_vma=False,
    )
```

```python
import jax
import jax.numpy as jnp
from jax import lax
from jax.experimental import pallas as pl
from jax.experimental.pallas import tpu as pltpu
from jax.sharding import Mesh
from jax.sharding import PartitionSpec as P

D = 512
HEADS = 16
HEAD_DIM = 32
WIN = 8
SHIFT = 4
NBIAS = 225
AREA = WIN * WIN
TOKENS = 128
GROUP = 4
SCALE = HEAD_DIM ** (-0.5)
EPSILON = 1e-05

F32 = jnp.float32
BF16 = jnp.bfloat16

PARTS = (("y", 8), ("zh", 2), ("core", 2), ("x", 4), ("zl", 6))
ROWS = ("y", "zh", "core")
COLS = ("x", "zl")
NROWS = 32
NCOLS = 24

ANY_PARAMS = pltpu.CompilerParams(vmem_limit_bytes=48 * 1024 * 1024)


def dot(a, b):
    return lax.dot_general(a, b, (((1,), (0,)), ((), ())), preferred_element_type=F32)


def dot_nt(a, b):
    return lax.dot_general(a, b, (((1,), (1,)), ((), ())), preferred_element_type=F32)


def dot_tn(a, b):
    return lax.dot_general(a, b, (((0,), (0,)), ((), ())), preferred_element_type=F32)


def iota(shape, dim):
    return lax.broadcasted_iota(jnp.int32, shape, dim)


def split_high_low(value):
    high = value.astype(BF16)
    low = (value - high.astype(F32)).astype(BF16)
    return high, low


def layer_stats(floats):
    average = jnp.mean(floats, axis=-1, keepdims=True)
    centred = floats - average
    variance = jnp.mean(centred * centred, axis=-1, keepdims=True)
    inv_std = lax.rsqrt(variance + EPSILON)
    return centred * inv_std, inv_std


def pack_kernel(tok, cot, reg, to_up, to_left, to_diag, tok_v, cot_v, reg_v, sem):
    copies = [
        pltpu.make_async_copy(src, dst, sem.at[k])
        for k, (src, dst) in enumerate(((tok, tok_v), (cot, cot_v), (reg, reg_v)))
    ]
    for copy in copies:
        copy.start()
    to_up[96:112] = jnp.zeros((16, D), BF16)
    to_left[8] = jnp.zeros((4, D), BF16)
    to_diag[8] = jnp.zeros((4, D), BF16)
    for copy in copies:
        copy.wait()
    for k, src in ((0, tok_v), (4, cot_v)):
        for r in range(0, SHIFT, 2):
            first = src[r].astype(F32)
            second = src[r + 1].astype(F32)
            at = (k + r) * 12
            to_up[at : at + 24] = jnp.concatenate([first[4:16], second[4:16]], axis=0).astype(BF16)
        for r in range(SHIFT):
            to_diag[k + r] = src[r].astype(F32)[0:4].astype(BF16)
            to_left[k + r] = src[SHIFT + r].astype(F32)[0:4].astype(BF16)
    classes = reg_v[...].astype(F32)
    to_up[96:104, 0:16] = classes.astype(BF16)
    to_diag[8, 0:4, 0:16] = classes[0:4].astype(BF16)
    to_left[8, 0:4, 0:16] = classes[4:8].astype(BF16)


def bias_kernel(
    table_far, bucket_far, wqkv_far, wout_far, bias, bucket2, wqkv, wout, table, bucket, sem
):
    copies = [
        pltpu.make_async_copy(table_far, table, sem.at[0]),
        pltpu.make_async_copy(bucket_far, bucket, sem.at[1]),
        pltpu.make_async_copy(wqkv_far, wqkv, sem.at[2]),
        pltpu.make_async_copy(wout_far, wout, sem.at[3]),
    ]
    for copy in copies:
        copy.start()
    for copy in copies[0:2]:
        copy.wait()
    turned = jnp.concatenate([table[...], jnp.zeros((HEADS, 256 - NBIAS), F32)], axis=1)
    both = jnp.concatenate([bucket[...], bucket[...]], axis=1)
    bucket2[...] = jnp.where(iota((32, 128), 1) < 64, both[0:32], both[32:64])
    for block in range(AREA // 8):
        index = both[block * 8 : block * 8 + 8]
        upper = index >= 128
        within = jnp.bitwise_and(index, 127)
        for h in range(HEADS):
            first = jnp.broadcast_to(turned[h : h + 1, 0:128], (8, 128))
            second = jnp.broadcast_to(turned[h : h + 1, 128:256], (8, 128))
            got_first = jnp.take_along_axis(first, within, axis=1, mode="promise_in_bounds")
            got_second = jnp.take_along_axis(second, within, axis=1, mode="promise_in_bounds")
            bias[h, block * 8 : block * 8 + 8, :] = jnp.where(upper, got_second, got_first)
    for copy in copies[2:]:
        copy.wait()


def window_kernel(
    tok_far, cot_far, reg_far, gain_far, wqkv, wout, bias, bucket2, up, diag, left,
    send, keep, own_grad, down_grad, right_grad, diag_grad,
    frame_t, frame_c, labels, packed, attended, grad_att, pairs, grad_in,
    tok, cot, reg, gain, sem,
):
    moves = ((tok_far, tok), (cot_far, cot), (reg_far, reg), (gain_far, gain))
    copies = [pltpu.make_async_copy(src, dst, sem.at[k]) for k, (src, dst) in enumerate(moves)]
    for copy in copies:
        copy.start()
    for copy in copies[0:3]:
        copy.wait()

    up_f = up[...].astype(F32)
    for src, k, frame in ((tok, 0, frame_t), (cot, 4, frame_c)):
        for r in range(SHIFT):
            own = src[SHIFT + r].astype(F32)
            frame[r * 8 : r * 8 + 8, :] = own[4:12]
            frame[64 + r * 8 : 64 + r * 8 + 4, :] = own[12:16]
            frame[64 + r * 8 + 4 : 64 + r * 8 + 8, :] = left[k + r].astype(F32)
            s = SHIFT + r
            below = up_f[(k + r) * 12 : (k + r) * 12 + 12]
            frame[s * 8 : s * 8 + 8, :] = below[0:8]
            frame[64 + s * 8 : 64 + s * 8 + 4, :] = below[8:12]
            frame[64 + s * 8 + 4 : 64 + s * 8 + 8, :] = diag[k + r].astype(F32)

    mine = reg[...].astype(F32)
    labels[...] = jnp.zeros_like(labels)
    labels[0:4, 0:12] = mine[4:8, 4:16]
    labels[0:4, 12:16] = left[8, 0:4, 0:16].astype(F32)[:, 0:4]
    labels[4:8, 0:12] = up_f[96:100, 4:16]
    labels[4:8, 12:16] = diag[8, 0:4, 0:16].astype(F32)[:, 0:4]
    row_tile = (lax.axis_index("y") * 2 + lax.axis_index("zh")) * 2 + lax.axis_index("core")
    last = (row_tile == NROWS - 1).astype(F32)
    flags = jnp.where(iota((8, 128), 0) >= 4, 2.0, 0.0) * last
    coded = labels[...] + flags + jnp.where(iota((8, 128), 1) >= 8, 4.0, 0.0)
    token_lane = iota((128, 128), 1)
    token_row = iota((128, 128), 0)

    def column_of(token):
        return (token // 64) * 8 + token % 8

    def row_of(token):
        return (token // 8) % 8

    pick_lane = (column_of(token_lane) == token_row).astype(BF16)
    wide = dot(coded.astype(BF16), pick_lane)
    code_row = jnp.sum(
        jnp.where(row_of(iota((8, 128), 1)) == iota((8, 128), 0), wide, 0.0), axis=0, keepdims=True
    )
    pick_row = (column_of(token_row) == token_lane).astype(BF16)
    padded_codes = jnp.concatenate([coded, jnp.zeros((120, 128), F32)], axis=0).astype(BF16)
    tall = dot_nt(pick_row, padded_codes)
    code_col = jnp.sum(
        jnp.where(row_of(token_row) == token_lane, tall, 0.0), axis=1, keepdims=True
    )
    allowed = jnp.broadcast_to(code_col, (128, 128)) == jnp.broadcast_to(code_row, (128, 128))
    allowed4 = jnp.concatenate([allowed.astype(F32)] * GROUP, axis=0) > 0.5

    hat, _ = layer_stats(frame_t[...])
    copies[3].wait()
    normed = (hat * gain[...]).astype(BF16)
    cots = frame_c[...].astype(BF16)
    packed[...] = dot(normed, wqkv[...]).astype(BF16)
    grad_att[...] = dot_nt(cots, wout[...]).astype(BF16)
    send[0:TOKENS, 3 * D : 4 * D] = cots

    lane_head = iota((TOKENS, 128), 1) // HEAD_DIM
    masks = [lane_head == h for h in range(GROUP)]

    def stacked(value):
        return jnp.concatenate(
            [jnp.where(m, value, jnp.zeros_like(value)) for m in masks], axis=0
        )

    def beside(value):
        return jnp.concatenate([value[h * 128 : h * 128 + 128] for h in range(GROUP)], axis=1)

    for g in range(HEADS // GROUP):
        at = g * 128
        query = packed[:, at : at + 128]
        key = packed[:, D + at : D + at + 128]
        value = packed[:, 2 * D + at : 2 * D + at + 128]
        outer = grad_att[:, at : at + 128]
        query_s = stacked(query)
        outer_s = stacked(outer)
        biases = []
        for h in range(GROUP):
            one = bias[g * GROUP + h]
            biases += [one, one]
        scores = dot_nt(query_s, key) * SCALE + jnp.concatenate(biases, axis=0)
        scores = jnp.where(allowed4, scores, -1e30)
        raised = jnp.exp(scores - jnp.max(scores, axis=-1, keepdims=True))
        probs = raised / jnp.sum(raised, axis=-1, keepdims=True)
        probs_low = probs.astype(BF16)
        grad_probs = dot_nt(outer_s, value)
        inner = probs * grad_probs
        grad_scores = probs * (grad_probs - jnp.sum(inner, axis=-1, keepdims=True))
        grad_scaled = (grad_scores * SCALE).astype(BF16)
        attended[:, at : at + 128] = dot(beside(probs_low), stacked(value)).astype(BF16)
        send[0:TOKENS, at : at + 128] = dot(beside(grad_scaled), stacked(key)).astype(BF16)
        send[0:TOKENS, D + at : D + at + 128] = dot_tn(grad_scaled, query_s).astype(BF16)
        send[0:TOKENS, 2 * D + at : 2 * D + at + 128] = dot_tn(probs_low, outer_s).astype(BF16)
        for h in range(GROUP):
            one = grad_scores[h * 128 : h * 128 + 128]
            pairs[g * GROUP + h] = (one[0:32] + one[96:128]) + pltpu.roll(
                one[32:64] + one[64:96], 64, 1
            )

    core = lax.axis_index("core")
    for k, matrix in ((0, normed), (1, attended[...])):
        turned = matrix.astype(F32).T.reshape(16, 2, 16, TOKENS)
        even, odd = turned[:, 0].reshape(256, TOKENS), turned[:, 1].reshape(256, TOKENS)
        kept = jnp.where(core == 0, even, odd).astype(BF16)
        sent = jnp.where(core == 0, odd, even).astype(BF16)
        for b in range(2):
            lane = (2 * k + b) * 128
            keep[:, lane : lane + 128] = kept[b * 128 : b * 128 + 128]
            send[0:TOKENS, 4 * D + lane : 4 * D + lane + 128] = sent[b * 128 : b * 128 + 128]

    grad_normed = dot_nt(send[0:TOKENS, 0 : 3 * D], wqkv[...])
    grad_in[...] = grad_normed
    gain_sum = jnp.sum(grad_normed * hat, axis=0, keepdims=True)

    bucket_of = iota((256, 128), 0)
    step = 2

    def add_rows(k, total):
        parts, hots = [], []
        for t in range(step):
            i = k * step + t
            parts.append(pairs[:, i, :])
            which = jnp.broadcast_to(bucket2[pl.ds(i, 1), :], (256, 128))
            hots.append((bucket_of == which).astype(BF16))
        high, low = split_high_low(jnp.concatenate(parts, axis=1))
        both = jnp.concatenate([high, low], axis=0)
        return total + dot_nt(both, jnp.concatenate(hots, axis=1))

    sums = lax.fori_loop(
        0, AREA // 2 // step, add_rows, jnp.zeros((2 * HEADS, 256), F32), unroll=True
    )
    table = sums[0:HEADS] + sums[HEADS : 2 * HEADS]
    high, low = split_high_low(table)
    send[TOKENS : TOKENS + 16, 0:256] = high
    send[TOKENS : TOKENS + 16, 256:512] = low
    high, low = split_high_low(jnp.concatenate([gain_sum, jnp.zeros((15, D), F32)], axis=0))
    send[TOKENS : TOKENS + 16, 512:1024] = high
    send[TOKENS : TOKENS + 16, 1024:1536] = low
    send[TOKENS : TOKENS + 16, 1536:2560] = jnp.zeros((16, 1024), BF16)

    for r in range(SHIFT):
        s = SHIFT + r
        own_grad[r, 0:8, :] = grad_in[r * 8 : r * 8 + 8, :]
        own_grad[r, 8:12, :] = grad_in[64 + r * 8 : 64 + r * 8 + 4, :]
        right_grad[r] = grad_in[64 + r * 8 : 64 + r * 8 + 8, :][4:8].astype(BF16)
        down_grad[r] = jnp.concatenate(
            [grad_in[s * 8 : s * 8 + 8, :], grad_in[64 + s * 8 : 64 + s * 8 + 8, :][0:4]], axis=0
        ).astype(BF16)
        diag_grad[r] = grad_in[64 + s * 8 : 64 + s * 8 + 8, :][4:8].astype(BF16)


def product_kernel(mine, other, keep, out):
    def rows(block):
        lane = block * 128
        return jnp.concatenate(
            [keep[:, lane : lane + 128], other[0:TOKENS, 4 * D + lane : 4 * D + lane + 128]], axis=1
        )

    right = jnp.concatenate([mine[0:TOKENS, 0 : 4 * D], other[0:TOKENS, 0 : 4 * D]], axis=0)
    for half in range(2):
        qkv = dot(rows(half), right[:, 0 : 3 * D]).astype(BF16)
        proj = dot(rows(2 + half), right[:, 3 * D : 4 * D]).astype(BF16)
        for k in range(4):
            for x in range(4):
                to = x * 8 + half * 4 + k
                at = k * 32
                for block in range(3):
                    lane = x * 384 + block * 128
                    out[to, block * 32 : block * 32 + 32, :] = qkv[at : at + 32, lane : lane + 128]
                out[to, 96:128, :] = proj[at : at + 32, x * 128 : x * 128 + 128]
    first = lax.axis_index("core") == 0
    small = mine[TOKENS : TOKENS + 16, 0:1536].astype(F32) + other[TOKENS : TOKENS + 16, 0:1536].astype(F32)
    table = small[:, 0:256] + small[:, 256:512]
    table = jnp.where(first, table[0:8], table[8:16])
    gain = small[0:8, 512:1024] + small[0:8, 1024:1536]
    gain = jnp.where(first, gain[:, 0:256], gain[:, 256:512])
    for x in range(4):
        lane = (x // 2) * 128
        piece = gain[:, lane : lane + 128]
        if x % 2 == 1:
            piece = pltpu.roll(piece, 64, 1)
        part = jnp.concatenate(
            [table[2 * x : 2 * x + 2, 0:128], table[2 * x : 2 * x + 2, 128:256], piece[0:4]], axis=0
        ).astype(BF16)
        for y in range(8):
            out[x * 8 + y, 128:136, :] = part


def plane_sum_kernel(parts, out):
    total = jnp.sum(parts[...].astype(F32), axis=0)
    left_half = iota((8, 128), 1) < 64
    small = total[128:136]
    for zh in range(2):
        proj = total[96 + zh * 16 : 112 + zh * 16].astype(BF16)
        for zl in range(6):
            at = (zl // 2) * 32 + zh * 16
            upper, lower = total[at : at + 8], total[at + 8 : at + 16]
            if zl % 2 == 0:
                lower = pltpu.roll(lower, 64, 1)
            else:
                upper = pltpu.roll(upper, 64, 1)
            qkv = jnp.where(left_half, upper, lower)
            out[zh * 6 + zl, 0:16, :] = proj
            out[zh * 6 + zl, 16:32, :] = jnp.concatenate([qkv, small], axis=0).astype(BF16)


def line_sum_kernel(parts, qkv, out):
    total = jnp.sum(parts[...].astype(F32), axis=0)
    qkv[0:8, :] = total[16:24, 0:64]
    qkv[8:16, :] = pltpu.roll(total[16:24], 64, 1)[:, 0:64]
    for to in range(8):
        out[to, 0:16, :] = total[0:16]
        out[to, 16:24, :] = total[24:32]


def finish_kernel(parts, proj, gain, table):
    core = lax.axis_index("core")
    for x in range(4):
        proj[:, x * 128 : x * 128 + 128] = parts[core * 4 + x, 0:16, :]
    left_half = iota((1, 128), 1) < 64
    low, high = [], []
    for k in range(8):
        low.append(parts[k, 16:18, :])
        high.append(parts[k, 18:20, :])
    for k in range(4):
        second = pltpu.roll(parts[2 * k + 1, 16:24, :], 64, 1)[4:5]
        gain[:, k * 128 : k * 128 + 128] = jnp.where(left_half, parts[2 * k, 20:21, :], second)
    table[:, 0:128] = jnp.concatenate(low, axis=0)
    table[:, 128:NBIAS] = jnp.concatenate(high, axis=0)[:, 0 : NBIAS - 128]


def token_kernel(tok, cot, gain, own, above, left, diag, out, grads):
    for r in range(SHIFT):
        grads[r, 0:4, :] = diag[r].astype(F32)
        grads[r, 4:16, :] = above[r].astype(F32)
        grads[SHIFT + r, 0:4, :] = left[r].astype(F32)
        grads[SHIFT + r, 4:16, :] = own[r]
    hat, inv_std = layer_stats(tok[...].astype(F32))
    grad_hat = grads[...] * gain[...].reshape(1, 1, D)
    moved = (
        grad_hat
        - jnp.mean(grad_hat, axis=-1, keepdims=True)
        - hat * jnp.mean(grad_hat * hat, axis=-1, keepdims=True)
    )
    out[...] = (cot[...].astype(F32) + inv_std * moved).astype(BF16)


def shape(dims, dtype):
    return jax.ShapeDtypeStruct(dims, dtype)


def call(kernel, outs, args, scratch=(), flops=0, moved=0, remain=(), params=ANY_PARAMS):
    args = [
        pltpu.with_memory_space_constraint(arg, pltpu.HBM) if k in remain else arg
        for k, arg in enumerate(args)
    ]
    return pl.pallas_call(
        kernel,
        in_specs=[
            pl.BlockSpec(memory_space=pltpu.HBM if k in remain else pltpu.VMEM)
            for k in range(len(args))
        ],
        out_shape=outs,
        scratch_shapes=list(scratch),
        compiler_params=params,
        cost_estimate=pl.CostEstimate(flops=flops, bytes_accessed=moved, transcendentals=0),
    )(*args)


def neighbour(value, down, right):
    pairs = [
        (r * NCOLS + c, ((r + down) % NROWS) * NCOLS + (c + right) % NCOLS)
        for r in range(NROWS)
        for c in range(NCOLS)
    ]
    return lax.ppermute(value, ROWS + COLS, pairs)


def local(tokens, cotangent, region, norm_gain, qkv_weight, out_weight, bias_table, bias_bucket):
    gain = norm_gain.reshape(1, D)
    to_up, to_left, to_diag = call(
        pack_kernel,
        [shape((112, D), BF16), shape((9, 4, D), BF16), shape((9, 4, D), BF16)],
        (tokens, cotangent, region),
        [
            pltpu.VMEM((8, 16, D), BF16),
            pltpu.VMEM((8, 16, D), BF16),
            pltpu.VMEM((8, 16), jnp.int32),
            pltpu.SemaphoreType.DMA((3,)),
        ],
        moved=1 << 19,
        remain=(0, 1, 2),
    )
    up = neighbour(to_up, -1, 0)
    left = neighbour(to_left, 0, -1)
    diag = neighbour(to_diag, -1, -1)
    bias, bucket2, wqkv, wout = call(
        bias_kernel,
        [
            shape((HEADS, AREA, 128), F32),
            shape((AREA // 2, 128), jnp.int32),
            shape((D, 3 * D), BF16),
            shape((D, D), BF16),
        ],
        (bias_table.T, bias_bucket, qkv_weight, out_weight),
        [
            pltpu.VMEM((HEADS, NBIAS), F32),
            pltpu.VMEM((AREA, AREA), jnp.int32),
            pltpu.SemaphoreType.DMA((4,)),
        ],
        moved=1 << 23,
        remain=(0, 1, 2, 3),
    )
    send, keep, own_grad, down_grad, right_grad, diag_grad = call(
        window_kernel,
        [
            shape((TOKENS + 16, 5 * D), BF16),
            shape((TOKENS, D), BF16),
            shape((4, 12, D), F32),
            shape((4, 12, D), BF16),
            shape((4, 4, D), BF16),
            shape((4, 4, D), BF16),
        ],
        (tokens, cotangent, region, gain, wqkv, wout, bias, bucket2, up, diag, left),
        [
            pltpu.VMEM((TOKENS, D), F32),
            pltpu.VMEM((TOKENS, D), F32),
            pltpu.VMEM((8, 128), F32),
            pltpu.VMEM((TOKENS, 3 * D), BF16),
            pltpu.VMEM((TOKENS, D), BF16),
            pltpu.VMEM((TOKENS, D), BF16),
            pltpu.VMEM((HEADS, AREA // 2, 128), F32),
            pltpu.VMEM((TOKENS, D), F32),
            pltpu.VMEM((8, 16, D), BF16),
            pltpu.VMEM((8, 16, D), BF16),
            pltpu.VMEM((8, 16), jnp.int32),
            pltpu.VMEM((1, D), F32),
            pltpu.SemaphoreType.DMA((4,)),
        ],
        flops=1 << 30,
        moved=1 << 23,
        remain=tuple(range(4)),
    )
    other = lax.ppermute(send, "core", [(0, 1), (1, 0)])
    products = call(
        product_kernel,
        shape((32, 136, 128), BF16),
        (send, other, keep),
        flops=1 << 29,
        moved=1 << 21,
    )
    products, down_grad, right_grad, diag_grad = lax.optimization_barrier(
        (products, down_grad, right_grad, diag_grad)
    )
    planes = lax.all_to_all(products, ("x", "y"), 0, 0)
    above_grad = neighbour(down_grad, 1, 0)
    left_grad = neighbour(right_grad, 0, 1)
    corner_grad = neighbour(diag_grad, 1, 1)
    chunks = call(plane_sum_kernel, shape((12, 32, 128), BF16), (planes,), moved=1 << 21)
    chunks, above_grad, left_grad, corner_grad = lax.optimization_barrier(
        (chunks, above_grad, left_grad, corner_grad)
    )
    lines = lax.all_to_all(chunks, ("zh", "zl"), 0, 0)
    grad_qkv, finals = call(
        line_sum_kernel, [shape((16, 64), F32), shape((8, 24, 128), F32)], (lines,), moved=1 << 18
    )
    finals = lax.all_to_all(finals, ("core", "x"), 0, 0)
    grad_tokens = call(
        token_kernel,
        shape((8, 16, D), BF16),
        (tokens, cotangent, gain, own_grad, above_grad, left_grad, corner_grad),
        [pltpu.VMEM((8, 16, D), F32)],
        moved=1 << 20,
    )
    grad_out_weight, grad_gain, grad_bias_table = call(
        finish_kernel,
        [shape((16, D), F32), shape((1, D), F32), shape((HEADS, NBIAS), F32)],
        (finals,),
        moved=1 << 17,
    )
    return (grad_tokens, grad_qkv, grad_out_weight, grad_gain.reshape(D), grad_bias_table.T)


def solution(mesh):
    parts = Mesh(mesh.devices.reshape([n for _, n in PARTS]), [name for name, _ in PARTS])
    return jax.shard_map(
        local,
        mesh=parts,
        in_specs=(P(ROWS, COLS, None), P(ROWS, COLS, None), P(ROWS, COLS), P(), P(), P(), P(), P()),
        out_specs=(P(ROWS, COLS, None), P(ROWS, COLS), P(ROWS, None), P(), P()),
        check_vma=False,
    )
```
